32 devices in a mesh: offset: 1, slab: 32 (over z, y, x, core).
Axes of the slice: x: 2, y: 2, z: 4, core: 2. Of those that a mesh axis runs over, the one named last changes fastest.
Arguments:
- traces: bfloat16 [1, 4096, 256], P('offset', 'slab'), may hold values from -6 to 6
- centre_ids: int32 [1, 4096, 1], P('offset', 'slab'), may hold values from 0 to 31; in each aligned block of 128 rows (0 to 127, 128 to 255, ..., all dimensions but the last counted through in order) at most 6 rows name the same one
- midpoint_bins: int32 [1, 4096], P('offset', 'slab'), may hold values from 0 to 15
- ray_times: float32 [1, 32, 7, 16, 256], P('offset', 'slab'), may hold values from 16 to 240
- ray_amps: float32 [1, 32, 7, 16, 256], P('offset', 'slab'), may hold values from 0.2 to 2
- beam_lateral: float32 [1, 32, 7, 16], P('offset'), may hold values from 0 to 128
- footprint: int32 [32, 7, 2], replicated, may hold values from 0 to 128, as said below
Outputs:
- image: float32 [256, 4096], P('offset', 'slab')
The draws below stay inside these ranges and needn't reach their ends.
Inputs may be any that keep to these rules, and one draw needn't show every extreme that they name: `centre_ids`: within the rows of one device no centre is named by more than 6 rows. footprint[c, w, 0] is below 64 and footprint[c, w, 1] above it; at w = 3, a centre's own slab, they are 0 and 128.
All inputs are finite; a program needn't handle non-finite values.
Results may differ from the reference program's by a relative error of at most 0.0049.
Values may be sent and summed in bfloat16 or wider, within the bound.
A program may use at most 64 MiB of HBM per device.

```python
import math
import jax
import jax.numpy as jnp
import numpy as np
from jax import lax

NT = 256
NF = 64
KLO = 8
P_SIZE = 16
BINS = 16
CAP = 6
WIN = 7
TRACE_DEV = 128
ZD = 256
XW = 128
CENTRES = 32
TRACES = 4096
OFFSETS = 1


def draw_footprint(key, part):
    key = jax.random.fold_in(key, 11)
    first_key, end_key = jax.random.split(key)
    first_col = jax.random.randint(first_key, (CENTRES, WIN), 0, XW // 2)
    end_col = jax.random.randint(end_key, (CENTRES, WIN), XW // 2 + 1, XW + 1)
    centre_slot = (jnp.arange(WIN) == (WIN - 1) // 2)[None, :]
    first_col = jnp.where(centre_slot, 0, first_col)
    end_col = jnp.where(centre_slot, XW, end_col)
    return jnp.stack([first_col, end_col], axis=-1).astype(jnp.int32)


def place_ends(array, own_key, smallest, largest):
    longest = array.shape.index(max(array.shape))
    spots = []
    for shift in (0, 1):
        where = [jax.random.randint(jax.random.fold_in(own_key, axis), (), 0, length) for axis, length in enumerate(array.shape)]
        where[longest] = (where[longest] + shift) % array.shape[longest]
        spots.append(tuple(where))
    return array.at[spots[0]].set(smallest).at[spots[1]].set(largest)


def level_of(own_key, shape, shards, smallest, high):
    def one(dim, shards_of):
        steps = jax.random.uniform(jax.random.fold_in(jax.random.fold_in(own_key, 6), dim), (shards_of,), jnp.float32, smallest / len(shards), high / len(shards))
        return jnp.repeat(jnp.exp(steps), shape[dim] // shards_of).reshape((-1,) + (1,) * (len(shape) - dim - 1))

    factor_of = one(*shards[0])
    for cut in shards[1:]:
        factor_of = factor_of * one(*cut)
    return factor_of


def shared_out(rng, own, number, rows, count, top, reach, lean):
    sequence = jax.random.permutation(rng, count)
    heavy_load, usual = portions_of(count, rows * top, reach, lean, True), portions_of(count, rows * top, reach, lean, False)
    places = jnp.arange(count)

    def named(lengths, offset_by):
        used = int((lengths > 0).sum())
        fixed = max(1, used // 4)
        passed = fixed + (places - fixed + offset_by * (used - fixed)) % max(1, count - fixed)
        return jnp.zeros((count,), jnp.int32).at[sequence[jnp.where(places < fixed, places, passed)]].set(jnp.asarray(lengths, jnp.int32))

    lengths = jnp.where(number % 4 == 0, named(heavy_load, number // 4), named(usual, number - number // 4 - 1))
    mixed = jax.random.permutation(jax.random.fold_in(own, 3), count)
    giver, receiver = mixed[0:count // 2 * 2:2], mixed[1:count // 2 * 2:2]
    slack = jnp.minimum(lengths[giver] - 1, reach - lengths[receiver]) // 2
    slack = jnp.where((giver == sequence[0]) | (receiver == sequence[0]) | (lengths[receiver] == 0), 0, jnp.maximum(slack, 0))
    passed = jax.random.randint(jax.random.fold_in(own, 4), (count // 2,), 0, 1 << 20) % (slack + 1)
    lengths = lengths.at[giver].add(-passed).at[receiver].add(passed)
    members = jnp.searchsorted(jnp.cumsum(lengths), jnp.arange(rows * top), side="right").astype(jnp.int32)
    listing = members.reshape(top, rows).T
    listing = listing[jax.random.permutation(jax.random.fold_in(own, 1), rows)]
    offset_by = jax.random.randint(jax.random.fold_in(own, 2), (rows, 1), 0, top)
    return jnp.take_along_axis(listing, (jnp.arange(top)[None, :] + offset_by) % top, axis=1)


def portions_of(count, total, limit, skew, full):
    portions = [(1 << 20) // math.isqrt(standing ** skew) + 1 for standing in range(1, count + 1)]
    largest = limit if full else min(limit, max(-(-total // count), total * portions[0] // sum(portions)))
    least = 1 if total - largest >= count - 1 else 0
    counts, surplus = [largest] + [least] * (count - 1), total - largest - least * (count - 1)
    while surplus > 0:
        movable = [i for i in range(1, count) if counts[i] < largest] or [i for i in range(1, count) if counts[i] < limit]
        whole, left = sum([portions[i] for i in movable]), surplus
        for i in movable:
            more = min(limit - counts[i], max(1, left * portions[i] // whole), surplus)
            counts[i] = counts[i] + more
            surplus = surplus - more
    return np.array(counts)


def normal_values(key, extent, scale, bound, cuts=(), kind=jnp.bfloat16):
    factor_of = level_of(key, extent, cuts, -0.22, 0.18) if cuts else 1.0
    array = jax.random.normal(key, extent, jnp.float32) * scale * factor_of
    return jnp.minimum(jnp.maximum(array, -bound), bound).astype(kind)


def setup_inputs(seed: int = 0) -> dict:
    streams_of = jax.random.split(jax.random.key(seed), 8)
    traces = normal_values(streams_of[0], (OFFSETS, TRACES, NT), 1.0, 6.0, ((1, 32),))
    centre_ids_keys = jax.random.split(jax.random.fold_in(streams_of[1], 1), OFFSETS * TRACES // TRACE_DEV)
    centre_ids_turns = jax.random.permutation(jax.random.fold_in(streams_of[1], 3), OFFSETS * TRACES // TRACE_DEV)
    centre_ids = jax.vmap(lambda own, number: shared_out(jax.random.fold_in(streams_of[1], 2), own, number, TRACE_DEV, CENTRES, 1, CAP, 1))(centre_ids_keys, centre_ids_turns).reshape((OFFSETS, TRACES, 1))
    midpoint_bins = place_ends(jax.random.randint(streams_of[2], (OFFSETS, TRACES), 0, BINS), jax.random.fold_in(streams_of[2], 1), 0, BINS - 1).astype(jnp.int32)
    ray_times = jnp.clip(16.0 + 224.0 * jax.random.uniform(streams_of[3], (OFFSETS, CENTRES, WIN, P_SIZE, ZD), jnp.float32) ** level_of(streams_of[3], (OFFSETS, CENTRES, WIN, P_SIZE, ZD), ((1, 32),), -0.2, 0.2), 16.0, 240.0)
    ray_amps = jnp.clip(jnp.exp(math.log(2.0) - 2.3025851 * jax.random.uniform(streams_of[4], (OFFSETS, CENTRES, WIN, P_SIZE, ZD), jnp.float32) ** level_of(streams_of[4], (OFFSETS, CENTRES, WIN, P_SIZE, ZD), ((1, 32),), -0.2, 0.2)), 0.2, 2.0)
    beam_lateral = jnp.clip(jax.random.uniform(streams_of[5], (OFFSETS, CENTRES, WIN, P_SIZE), jnp.float32, 0.0, 128.0), 0.0, 128.0)
    footprint = draw_footprint(jax.random.fold_in(streams_of[7], 71), 0)
    return {"traces": traces, "centre_ids": centre_ids, "midpoint_bins": midpoint_bins, "ray_times": ray_times, "ray_amps": ray_amps, "beam_lateral": beam_lateral, "footprint": footprint}


two_pi = 2.0 * math.pi
slow_step = 0.25
width_scale = 200.0

def dft_table():
    sample = jnp.arange(NT, dtype=jnp.int32)[:, None]
    bin_index = jnp.arange(NF, dtype=jnp.int32)[None, :] + KLO
    turns = (sample * bin_index % NT).astype(jnp.float32) * (two_pi / NT)
    return jnp.concatenate([jnp.cos(turns), -jnp.sin(turns)], axis=1)

def omegas():
    return (jnp.arange(NF, dtype=jnp.int32) + KLO).astype(jnp.float32) * (two_pi / NT)

def slowness():
    return (jnp.arange(P_SIZE, dtype=jnp.int32).astype(jnp.float32) - (P_SIZE - 1) / 2.0) * slow_step

def slant_terms(spectrum, places):
    phase = omegas()[None, None, :] * slowness()[None, :, None] * places[:, None, None]
    cosine = jnp.cos(phase)
    sine_part = jnp.sin(phase)
    spec_re = spectrum[:, None, :NF]
    spec_im = spectrum[:, None, NF:]
    return (spec_re * cosine + spec_im * sine_part, spec_im * cosine - spec_re * sine_part)

def beam_blocks(beams, times_in, amps_in, lateral, first_col, end_col):
    freq = omegas()
    phase = freq[None, :, None] * times_in[:, None, :]
    depth = times_in.shape[1]
    u_block = jnp.stack([amps_in[:, None, :] * jnp.cos(phase), -amps_in[:, None, :] * jnp.sin(phase)])
    u_block = u_block.reshape(2 * P_SIZE * NF, depth).astype(jnp.bfloat16)
    col_index = jnp.arange(XW, dtype=jnp.int32)
    inside = ((col_index >= first_col) & (col_index < end_col)).astype(jnp.float32)
    columns = col_index.astype(jnp.float32)
    gauss = jnp.exp(-(columns[None, None, :] - lateral[:, None, None]) ** 2 * freq[None, :, None] / width_scale)
    gauss = gauss * inside[None, None, :] / math.sqrt(P_SIZE * NF)
    beam_re = beams[:, :NF].astype(jnp.float32)[:, :, None]
    beam_im = beams[:, NF:].astype(jnp.float32)[:, :, None]
    v_block = jnp.stack([beam_re * gauss, beam_im * gauss]).reshape(2 * P_SIZE * NF, XW).astype(jnp.bfloat16)
    return (u_block, v_block)

def reference(traces, centre_ids, midpoint_bins, ray_times, ray_amps, beam_lateral, footprint):
    table = dft_table()
    half_win = (WIN - 1) // 2
    scale = 1.0 / math.sqrt(NT * TRACE_DEV)

    def one_group(group):
        group_traces, group_ids, group_bins, group_times, group_amps, group_lateral = group
        spectrum = jnp.dot(group_traces.astype(jnp.float32), table, precision=lax.Precision.HIGHEST)
        places = group_bins.astype(jnp.float32) - (BINS - 1) / 2.0
        terms_re, terms_im = slant_terms(spectrum, places)
        beam_re = jax.ops.segment_sum(terms_re, group_ids[:, 0], CENTRES)
        beam_im = jax.ops.segment_sum(terms_im, group_ids[:, 0], CENTRES)
        beams = (jnp.concatenate([beam_re, beam_im], axis=2) * scale).astype(jnp.bfloat16)

        def per_centre(centre, accum):
            for window in range(WIN):
                target = centre + window - half_win
                valid = ((target >= 0) & (target < CENTRES)).astype(jnp.float32)
                u_block, v_block = beam_blocks(beams[centre], group_times[centre, window], group_amps[centre, window], group_lateral[centre, window], footprint[centre, window, 0], footprint[centre, window, 1])
                contrib = lax.dot_general(u_block.astype(jnp.float32), v_block.astype(jnp.float32), (((0,), (0,)), ((), ())), precision=lax.Precision.HIGHEST)
                slot = jnp.clip(target, 0, CENTRES - 1).astype(jnp.int32)
                accum = accum.at[:, slot].add(contrib * valid)
            return accum
        start = jnp.zeros((ZD, CENTRES, XW), jnp.float32)
        return lax.fori_loop(0, CENTRES, per_centre, start)
    images = lax.map(one_group, (traces, centre_ids, midpoint_bins, ray_times, ray_amps, beam_lateral))
    return lax.optimization_barrier(jnp.sum(images, axis=0)).reshape(ZD, CENTRES * XW)
```

```python
import functools
import math

import jax
import jax.numpy as jnp
import ml_dtypes
import numpy as np
from jax import lax
from jax.experimental import pallas as pl
from jax.experimental.pallas import tpu as pltpu
from jax.sharding import PartitionSpec as P

NT = 256
NF = 64
KLO = 8
P_SIZE = 16
BINS = 16
WIN = 7
XW = 128
HALF = (WIN - 1) // 2
STEPS = NF // KLO
LANES = KLO * P_SIZE

slow_step = 0.25
width_scale = 200.0

ORDER = (3, 2, 4, 1, 5, 0, 6)


def halves(table):
    high = table.astype(ml_dtypes.bfloat16)
    low = (table - high.astype(np.float64)).astype(ml_dtypes.bfloat16)
    return high, low


def dft_halves():
    turns = np.outer(np.arange(NT), np.arange(NF) + KLO) % NT * (2.0 * np.pi / NT)
    return np.concatenate(halves(np.concatenate([np.cos(turns), -np.sin(turns)], axis=1)), axis=1)


def slant_halves():
    omega = (np.arange(NF) + KLO) * (2.0 * np.pi / NT)
    slow = (np.arange(P_SIZE) - (P_SIZE - 1) / 2.0) * slow_step
    place = np.arange(BINS) - (BINS - 1) / 2.0
    phase = place[:, None] * (omega[:, None] * slow[None, :]).reshape(1, -1)
    return np.concatenate(halves(np.concatenate([np.cos(phase), np.sin(phase)], axis=1)), axis=0)


def fit_even(values, degree):
    nodes = 0.125 - 0.125 * np.cos((np.arange(400) + 0.5) * np.pi / 400)
    poly = np.polynomial.chebyshev.Chebyshev.fit(nodes, values(np.sqrt(nodes)), degree, domain=[0, 0.25])
    return [float(c) for c in poly.convert(kind=np.polynomial.Polynomial).coef]


COS_FIT = fit_even(lambda y: np.cos(2 * np.pi * y), 7)
SIN_FIT = fit_even(lambda y: np.sin(2 * np.pi * y) / y, 6)


def horner(fit, s):
    total = jnp.full_like(s, fit[-1])
    for c in fit[-2::-1]:
        total = total * s + c
    return total


def turn(y):
    y = y - jnp.floor(y + 0.5)
    s = y * y
    return horner(COS_FIT, s), horner(SIN_FIT, s) * y


def kernel(
    slabs, scale,
    traces, centre_ids, bins, dft, slant, times, amps, lateral, footprint,
    image,
    spread, sums, send, arrived, ray_t, ray_a, beams, u, v, gauss, step, total,
    send_sem, recv_sem, ray_send, ray_recv, beam_send, beam_recv,
):
    me = lax.axis_index("slab")

    def slab_at(k):
        return lax.rem(me + k, slabs)

    barrier = pltpu.get_barrier_semaphore()

    def greet(k, carry):
        pl.semaphore_signal(barrier, inc=1, device_id={"slab": slab_at(k)}, device_id_type=pl.DeviceIdType.MESH)
        return carry

    lax.fori_loop(1, slabs, greet, 0)

    spectrum = jnp.dot(traces[0], dft[...], preferred_element_type=jnp.float32)
    spectrum = spectrum[:, : 2 * NF] + spectrum[:, 2 * NF :]
    spec_high = spectrum.astype(jnp.bfloat16)
    spec_low = (spectrum - spec_high.astype(jnp.float32)).astype(jnp.bfloat16)
    spec = jnp.concatenate([spec_high, spec_low], axis=1)
    count = spec.shape[0]
    row = lax.broadcasted_iota(jnp.int32, (2 * NF, 2 * NF * P_SIZE), 0)
    column = lax.broadcasted_iota(jnp.int32, (2 * NF, 2 * NF * P_SIZE), 1)
    one_of = jnp.where(row == column // P_SIZE, 1.0, 0.0).astype(jnp.bfloat16)
    spread[: 2 * NF] = one_of
    spread[2 * NF :] = one_of
    bin_row = lax.rem(lax.broadcasted_iota(jnp.int32, (2 * BINS, count), 0), BINS)
    bin_hot = jnp.where(bin_row == bins[...], 1.0, 0.0).T.astype(jnp.bfloat16)
    id_row = lax.broadcasted_iota(jnp.int32, (slabs, count), 0)
    id_hot = jnp.where(id_row == centre_ids[...], 1.0, 0.0)
    id_hot = id_hot.astype(jnp.bfloat16)
    id_hot = jnp.concatenate([id_hot, id_hot], axis=1)
    for chunk in range(STEPS):
        re_at = slice(chunk * LANES, (chunk + 1) * LANES)
        im_at = slice((STEPS + chunk) * LANES, (STEPS + chunk + 1) * LANES)
        spec_re = jnp.dot(spec, spread[:, re_at], preferred_element_type=jnp.float32)
        spec_im = jnp.dot(spec, spread[:, im_at], preferred_element_type=jnp.float32)
        cosine = jnp.dot(bin_hot, slant[:, re_at], preferred_element_type=jnp.float32)
        sine = jnp.dot(bin_hot, slant[:, im_at], preferred_element_type=jnp.float32)
        terms = jnp.concatenate(
            [spec_re * cosine + spec_im * sine, spec_im * cosine - spec_re * sine], axis=1
        )
        high = terms.astype(jnp.bfloat16)
        low = (terms - high.astype(jnp.float32)).astype(jnp.bfloat16)
        partial = jnp.dot(
            id_hot, jnp.concatenate([high, low], axis=0), preferred_element_type=jnp.float32
        )
        sums[:, 2 * chunk, :] = partial[:, :LANES] * scale
        sums[:, 2 * chunk + 1, :] = partial[:, LANES:] * scale
    send[...] = sums[...].astype(jnp.bfloat16)

    pl.semaphore_wait(barrier, slabs - 1)

    def block_copy(k):
        return pltpu.make_async_remote_copy(
            src_ref=send.at[slab_at(k)],
            dst_ref=arrived.at[k],
            send_sem=send_sem.at[k],
            recv_sem=recv_sem.at[k],
            device_id={"slab": slab_at(k)},
            device_id_type=pl.DeviceIdType.MESH,
        )

    def start_block(k, carry):
        block_copy(k).start()
        return carry

    def ray_copies(w):
        target = {"slab": slab_at(slabs + w - HALF)}
        return [
            pltpu.make_async_remote_copy(
                src_ref=source.at[0, 0, w],
                dst_ref=held.at[w],
                send_sem=ray_send.at[i, w],
                recv_sem=ray_recv.at[i, w],
                device_id=target,
                device_id_type=pl.DeviceIdType.MESH,
            )
            for i, (source, held) in enumerate(((times, ray_t), (amps, ray_a)))
        ]

    def beam_copy(w):
        return pltpu.make_async_remote_copy(
            src_ref=beams.at[HALF],
            dst_ref=beams.at[w],
            send_sem=beam_send.at[w],
            recv_sem=beam_recv.at[w],
            device_id={"slab": slab_at(slabs + w - HALF)},
            device_id_type=pl.DeviceIdType.MESH,
        )

    def goes(w):
        target = me + (w - HALF)
        return (target >= 0) & (target < slabs)

    def comes(w):
        source = me - (w - HALF)
        return (source >= 0) & (source < slabs)

    for w in ORDER[1:]:

        @pl.when(goes(w))
        def _():
            for copy in ray_copies(w):
                copy.start()

    lax.fori_loop(1, slabs, start_block, 0)

    def make_u(w, t, a):
        cos8, sin8 = turn(t * (KLO / NT))
        cos1, sin1 = turn(t * (1.0 / NT))
        twice = 2.0 * cos8
        re, im = a, jnp.zeros_like(a)
        for b in range(KLO):
            if b:
                re, im = re * cos1 + im * sin1, im * cos1 - re * sin1
            last_re, last_im = re, im
            now_re, now_im = re * cos8 + im * sin8, im * cos8 - re * sin8
            for chunk in range(STEPS):
                at = 2 * chunk * LANES + b * P_SIZE
                u[w, at : at + P_SIZE, :] = now_re.astype(jnp.bfloat16)
                u[w, at + LANES : at + LANES + P_SIZE, :] = now_im.astype(jnp.bfloat16)
                if chunk < STEPS - 1:
                    now_re, last_re = twice * now_re - last_re, now_re
                    now_im, last_im = twice * now_im - last_im, now_im

    lane = lax.broadcasted_iota(jnp.int32, (1, LANES), 1)
    place = lax.broadcasted_iota(jnp.int32, (XW, LANES), 0)
    rate = -2.0 * math.pi / NT / width_scale * math.log2(math.e)
    rates = (lane // P_SIZE + KLO).astype(jnp.float32) * rate

    def make_gauss(w):
        centre = jnp.clip(me - (w - HALF), 0, slabs - 1)
        axis = lateral[0, centre, w : w + 1, :]
        axis = jnp.concatenate([axis] * KLO, axis=1)
        first, end = footprint[centre, w, 0], footprint[centre, w, 1]
        off = place.astype(jnp.float32) - axis
        off = jnp.where((place >= first) & (place < end), off * off, 1e9)
        gauss[w] = jnp.exp2(off * rates) * (1.0 / math.sqrt(P_SIZE * NF))
        step[w] = jnp.exp2(off * (KLO * rate))

    def add_slot(w):
        here = beams[w].astype(jnp.float32)
        g = gauss[w]
        for chunk in range(STEPS):
            if chunk:
                g = g * step[w]
            at = 2 * chunk * LANES
            v[:, at : at + LANES] = (g * here[2 * chunk : 2 * chunk + 1]).astype(jnp.bfloat16)
            v[:, at + LANES : at + 2 * LANES] = (g * here[2 * chunk + 1 : 2 * chunk + 2]).astype(
                jnp.bfloat16
            )
        return jnp.dot(v[...], u[w], preferred_element_type=jnp.float32)

    make_u(HALF, times[0, 0, HALF], amps[0, 0, HALF])
    for w in ORDER:
        make_gauss(w)
    for w in ORDER[1:]:

        @pl.when(comes(w))
        def _():
            for copy in ray_copies(w):
                copy.wait_recv()
            make_u(w, ray_t[w], ray_a[w])

    def take_block(k, carry):
        block_copy(k).wait_recv()
        return carry + arrived[k].astype(jnp.float32)

    own = lax.fori_loop(1, slabs, take_block, send[me].astype(jnp.float32))
    beams[HALF] = own.astype(jnp.bfloat16)
    for w in ORDER[1:]:

        @pl.when(goes(w))
        def _():
            beam_copy(w).start()

    total[...] = add_slot(HALF)
    for w in ORDER[1:]:

        @pl.when(comes(w))
        def _():
            beam_copy(w).wait_recv()
            total[...] += add_slot(w)

    image[...] = total[...].T

    def sent_block(k, carry):
        block_copy(k).wait_send()
        return carry

    lax.fori_loop(1, slabs, sent_block, 0)
    for w in ORDER[1:]:

        @pl.when(goes(w))
        def _():
            for copy in ray_copies(w):
                copy.wait_send()
            beam_copy(w).wait_send()


def shards(traces, centre_ids, midpoint_bins, ray_times, ray_amps, beam_lateral, footprint):
    slabs = lax.axis_size("slab")
    count = traces.shape[1]
    depth = ray_times.shape[4]
    vmem = pl.BlockSpec(memory_space=pltpu.VMEM)
    smem = pl.BlockSpec(memory_space=pltpu.SMEM)
    partial_image = pl.pallas_call(
        functools.partial(kernel, slabs, 1.0 / math.sqrt(NT * count)),
        out_shape=jax.ShapeDtypeStruct((depth, XW), jnp.float32),
        in_specs=[vmem] * 8 + [smem],
        out_specs=vmem,
        scratch_shapes=[
            pltpu.VMEM((4 * NF, 2 * NF * P_SIZE), jnp.bfloat16),
            pltpu.VMEM((slabs, 2 * STEPS, LANES), jnp.float32),
            pltpu.VMEM((slabs, 2 * STEPS, LANES), jnp.bfloat16),
            pltpu.VMEM((slabs, 2 * STEPS, LANES), jnp.bfloat16),
            pltpu.VMEM((WIN, P_SIZE, depth), jnp.float32),
            pltpu.VMEM((WIN, P_SIZE, depth), jnp.float32),
            pltpu.VMEM((WIN, 2 * STEPS, LANES), jnp.bfloat16),
            pltpu.VMEM((WIN, 2 * NF * P_SIZE, depth), jnp.bfloat16),
            pltpu.VMEM((XW, 2 * NF * P_SIZE), jnp.bfloat16),
            pltpu.VMEM((WIN, XW, LANES), jnp.float32),
            pltpu.VMEM((WIN, XW, LANES), jnp.float32),
            pltpu.VMEM((XW, depth), jnp.float32),
            pltpu.SemaphoreType.DMA((slabs,)),
            pltpu.SemaphoreType.DMA((slabs,)),
            pltpu.SemaphoreType.DMA((2, WIN)),
            pltpu.SemaphoreType.DMA((2, WIN)),
            pltpu.SemaphoreType.DMA((WIN,)),
            pltpu.SemaphoreType.DMA((WIN,)),
        ],
        compiler_params=pltpu.CompilerParams(
            collective_id=0, has_side_effects=True, vmem_limit_bytes=40 * 1024 * 1024
        ),
    )(
        traces,
        centre_ids.reshape(1, count),
        midpoint_bins,
        jnp.asarray(dft_halves()),
        jnp.asarray(slant_halves()),
        ray_times,
        ray_amps,
        beam_lateral,
        footprint,
    )
    if lax.axis_size("offset") == 1:
        return partial_image
    return lax.psum_scatter(partial_image, "offset", scatter_dimension=0, tiled=True)


def solution(mesh):
    return jax.shard_map(
        shards,
        mesh=mesh,
        in_specs=(
            P("offset", "slab", None),
            P("offset", "slab", None),
            P("offset", "slab"),
            P("offset", "slab", None, None, None),
            P("offset", "slab", None, None, None),
            P("offset", None, None, None),
            P(),
        ),
        out_specs=P("offset", "slab"),
        check_vma=False,
    )
```

```python
import functools
import math

import jax
import jax.numpy as jnp
import ml_dtypes
import numpy as np
from jax import lax
from jax.experimental import pallas as pl
from jax.experimental.pallas import tpu as pltpu
from jax.sharding import PartitionSpec as P

NT = 256
NF = 64
KLO = 8
P_SIZE = 16
BINS = 16
WIN = 7
XW = 128
HALF = (WIN - 1) // 2
STEPS = NF // KLO
LANES = KLO * P_SIZE

slow_step = 0.25
width_scale = 200.0

ORDER = (3, 2, 4, 1, 5, 0, 6)


def halves(table):
    high = table.astype(ml_dtypes.bfloat16)
    low = (table - high.astype(np.float64)).astype(ml_dtypes.bfloat16)
    return high, low


def dft_halves():
    turns = np.outer(np.arange(NT), np.arange(NF) + KLO) % NT * (2.0 * np.pi / NT)
    return np.concatenate(halves(np.concatenate([np.cos(turns), -np.sin(turns)], axis=1)), axis=1)


def by_chunk(table):
    rows = table.shape[0]
    return table.reshape(rows, 2, STEPS, LANES).transpose(0, 2, 1, 3).reshape(rows, -1)


def slant_halves():
    omega = (np.arange(NF) + KLO) * (2.0 * np.pi / NT)
    slow = (np.arange(P_SIZE) - (P_SIZE - 1) / 2.0) * slow_step
    place = np.arange(BINS) - (BINS - 1) / 2.0
    phase = place[:, None] * (omega[:, None] * slow[None, :]).reshape(1, -1)
    table = by_chunk(np.concatenate([np.cos(phase), np.sin(phase)], axis=1))
    return np.concatenate(halves(table), axis=0)


def spread_table():
    one_of = by_chunk(np.repeat(np.eye(2 * NF), P_SIZE, axis=1))
    return np.concatenate([one_of, one_of], axis=0).astype(ml_dtypes.bfloat16)


def fit_even(values, degree):
    nodes = 0.125 - 0.125 * np.cos((np.arange(400) + 0.5) * np.pi / 400)
    poly = np.polynomial.chebyshev.Chebyshev.fit(nodes, values(np.sqrt(nodes)), degree, domain=[0, 0.25])
    return [float(c) for c in poly.convert(kind=np.polynomial.Polynomial).coef]


COS_FIT = fit_even(lambda y: np.cos(2 * np.pi * y), 7)
SIN_FIT = fit_even(lambda y: np.sin(2 * np.pi * y) / y, 6)


def horner(fit, s):
    total = jnp.full_like(s, fit[-1])
    for c in fit[-2::-1]:
        total = total * s + c
    return total


def turn(y):
    y = y - jnp.floor(y + 0.5)
    s = y * y
    return horner(COS_FIT, s), horner(SIN_FIT, s) * y


def kernel(
    slabs, scale,
    traces_in, ids_in, bins_in, dft_in, slant_in, spread_in, times_in, amps_in, lateral_in, footprint_in,
    image,
    traces, ids, bins, dft, slant, spread, lateral, footprint,
    rays, rays_here, sums, send, arrived, beams, u, v, gauss, step,
    load_sem, send_sem, recv_sem, ray_send, ray_recv, beam_send, beam_recv,
):
    me = lax.axis_index("slab")

    def slab_at(k):
        return lax.rem(me + k, slabs)

    loads = [
        pltpu.make_async_copy(source, held, load_sem.at[i])
        for i, (source, held) in enumerate(
            (
                (traces_in.at[0], traces),
                (dft_in, dft),
                (ids_in, ids),
                (bins_in, bins),
                (slant_in, slant),
                (spread_in, spread),
                (times_in.at[0, 0], rays.at[:, 0]),
                (amps_in.at[0, 0], rays.at[:, 1]),
                (lateral_in.at[0], lateral),
                (footprint_in, footprint),
            )
        )
    ]
    for load in loads:
        load.start()

    barrier = pltpu.get_barrier_semaphore()

    def greet(k, carry):
        pl.semaphore_signal(barrier, inc=1, device_id={"slab": slab_at(k)}, device_id_type=pl.DeviceIdType.MESH)
        return carry

    lax.fori_loop(1, slabs, greet, 0)

    def block_copies(first, count):
        return pltpu.make_async_remote_copy(
            src_ref=send.at[pl.ds(slab_at(first), count)] if count == 1 else send.at[pl.ds(0, count)],
            dst_ref=arrived.at[pl.ds(first, count)],
            send_sem=send_sem,
            recv_sem=recv_sem,
            device_id={"slab": slab_at(first)},
            device_id_type=pl.DeviceIdType.MESH,
        )

    def start_block(k, carry):
        block_copies(k, 1).start()
        return carry

    def ray_copy(w):
        return pltpu.make_async_remote_copy(
            src_ref=rays.at[w],
            dst_ref=rays_here.at[w],
            send_sem=ray_send.at[w],
            recv_sem=ray_recv.at[w],
            device_id={"slab": slab_at(slabs + w - HALF)},
            device_id_type=pl.DeviceIdType.MESH,
        )

    def beam_copy(w):
        return pltpu.make_async_remote_copy(
            src_ref=beams.at[HALF],
            dst_ref=beams.at[w],
            send_sem=beam_send.at[w],
            recv_sem=beam_recv.at[w],
            device_id={"slab": slab_at(slabs + w - HALF)},
            device_id_type=pl.DeviceIdType.MESH,
        )

    def goes(w):
        target = me + (w - HALF)
        return (target >= 0) & (target < slabs)

    def comes(w):
        source = me - (w - HALF)
        return (source >= 0) & (source < slabs)

    for load in loads[:4]:
        load.wait()
    spectrum = jnp.dot(traces[...], dft[...], preferred_element_type=jnp.float32)
    spectrum = spectrum[:, : 2 * NF] + spectrum[:, 2 * NF :]
    spec_high = spectrum.astype(jnp.bfloat16)
    spec_low = (spectrum - spec_high.astype(jnp.float32)).astype(jnp.bfloat16)
    spec = jnp.concatenate([spec_high, spec_low], axis=1)
    count = spec.shape[0]
    bin_row = lax.broadcasted_iota(jnp.int32, (2 * BINS, count), 0) % BINS
    bin_hot = jnp.where(bin_row == bins[...], 1.0, 0.0).T.astype(jnp.bfloat16)
    id_row = lax.broadcasted_iota(jnp.int32, (slabs, count), 0)
    id_hot = jnp.where(id_row == ids[...], 1.0, 0.0).astype(jnp.bfloat16)
    id_hot = jnp.concatenate([id_hot, id_hot], axis=1)
    for load in loads[4:8]:
        load.wait()

    pl.semaphore_wait(barrier, slabs - 1)
    for w in ORDER[1:]:

        @pl.when(goes(w))
        def _():
            ray_copy(w).start()

        @pl.when(jnp.logical_not(comes(w)))
        def _():
            rays_here[w] = rays[w]
            beams[w] = jnp.zeros_like(beams[w])

    for chunk in range(STEPS):
        at = slice(2 * chunk * LANES, 2 * (chunk + 1) * LANES)
        spec_wide = jnp.dot(spec, spread[:, at], preferred_element_type=jnp.float32)
        turn_wide = jnp.dot(bin_hot, slant[:, at], preferred_element_type=jnp.float32)
        spec_re, spec_im = spec_wide[:, :LANES], spec_wide[:, LANES:]
        cosine, sine = turn_wide[:, :LANES], turn_wide[:, LANES:]
        terms = jnp.concatenate(
            [spec_re * cosine + spec_im * sine, spec_im * cosine - spec_re * sine], axis=1
        )
        high = terms.astype(jnp.bfloat16)
        low = (terms - high.astype(jnp.float32)).astype(jnp.bfloat16)
        partial = jnp.dot(
            id_hot, jnp.concatenate([high, low], axis=0), preferred_element_type=jnp.float32
        )
        sums[:, 2 * chunk, :] = partial[:, :LANES] * scale
        sums[:, 2 * chunk + 1, :] = partial[:, LANES:] * scale
    send[...] = sums[...].astype(jnp.bfloat16)
    lax.fori_loop(1, slabs, start_block, 0)

    def make_u(w, t, a):
        cos8, sin8 = turn(t * (KLO / NT))
        cos1, sin1 = turn(t * (1.0 / NT))
        twice = 2.0 * cos8
        re, im = a, jnp.zeros_like(a)
        for b in range(KLO):
            if b:
                re, im = re * cos1 + im * sin1, im * cos1 - re * sin1
            last_re, last_im = re, im
            now_re, now_im = re * cos8 + im * sin8, im * cos8 - re * sin8
            for chunk in range(STEPS):
                at = 2 * chunk * LANES + b * P_SIZE
                u[w, at : at + P_SIZE, :] = now_re.astype(jnp.bfloat16)
                u[w, at + LANES : at + LANES + P_SIZE, :] = now_im.astype(jnp.bfloat16)
                if chunk < STEPS - 1:
                    now_re, last_re = twice * now_re - last_re, now_re
                    now_im, last_im = twice * now_im - last_im, now_im

    lane = lax.broadcasted_iota(jnp.int32, (1, LANES), 1)
    place = lax.broadcasted_iota(jnp.int32, (XW, LANES), 0).astype(jnp.float32)
    slow_row = lax.broadcasted_iota(jnp.int32, (P_SIZE, LANES), 0)
    slow_lane = lax.broadcasted_iota(jnp.int32, (P_SIZE, LANES), 1) % P_SIZE
    rate = -2.0 * math.pi / NT / width_scale * math.log2(math.e)
    rates = (lane // P_SIZE + KLO).astype(jnp.float32) * rate

    def pick(values, w):
        centre = jnp.clip(me - (w - HALF), 0, slabs - 1)
        held = lax.broadcasted_iota(jnp.int32, values.shape, 1) == centre
        return jnp.sum(jnp.where(held, values, 0.0), axis=1, keepdims=True)

    def make_gauss(w):
        axis = pick(lateral[w], w)
        axis = jnp.sum(jnp.where(slow_row == slow_lane, axis, 0.0), axis=0, keepdims=True)
        ends = pick(footprint[w].astype(jnp.float32), w)
        off = place - axis
        off = jnp.where((place >= ends[0:1]) & (place < ends[1:2]), off * off, 1e9)
        gauss[w] = jnp.exp2(off * rates) * (1.0 / math.sqrt(P_SIZE * NF))
        step[w] = jnp.exp2(off * (KLO * rate))

    def slot_image(w):
        here = beams[w].astype(jnp.float32)
        g = gauss[w]
        for chunk in range(STEPS):
            if chunk:
                g = g * step[w]
            at = 2 * chunk * LANES
            v[w, :, at : at + LANES] = (g * here[2 * chunk : 2 * chunk + 1]).astype(jnp.bfloat16)
            v[w, :, at + LANES : at + 2 * LANES] = (
                g * here[2 * chunk + 1 : 2 * chunk + 2]
            ).astype(jnp.bfloat16)
        return jnp.dot(v[w], u[w], preferred_element_type=jnp.float32)

    def take_rays(w):
        @pl.when(comes(w))
        def _():
            ray_copy(w).wait_recv()

        make_u(w, rays_here[w, 0], rays_here[w, 1])

    make_u(HALF, rays[HALF, 0], rays[HALF, 1])
    for load in loads[8:]:
        load.wait()
    for w in ORDER:
        make_gauss(w)
    for w in ORDER[1:5]:
        take_rays(w)

    arrived[0] = send[me]
    block_copies(1, slabs - 1).wait_recv()
    own = jnp.sum(arrived[...].astype(jnp.float32), axis=0)
    beams[HALF] = own.astype(jnp.bfloat16)
    for w in ORDER[1:]:

        @pl.when(goes(w))
        def _():
            beam_copy(w).start()

    for w in ORDER[5:]:
        take_rays(w)
    total = slot_image(HALF)
    for w in ORDER[1:]:

        @pl.when(comes(w))
        def _():
            beam_copy(w).wait_recv()

    for w in ORDER[1:]:
        total += slot_image(w)
    image[...] = total.T

    block_copies(1, slabs - 1).wait_send()
    for w in ORDER[1:]:

        @pl.when(goes(w))
        def _():
            ray_copy(w).wait_send()
            beam_copy(w).wait_send()


def shards(traces, centre_ids, midpoint_bins, ray_times, ray_amps, beam_lateral, footprint):
    slabs = lax.axis_size("slab")
    count = traces.shape[1]
    depth = ray_times.shape[4]
    columns = 2 * NF * P_SIZE
    partial_image = pl.pallas_call(
        functools.partial(kernel, slabs, 1.0 / math.sqrt(NT * count)),
        out_shape=jax.ShapeDtypeStruct((depth, XW), jnp.float32),
        in_specs=[pl.BlockSpec(memory_space=pltpu.HBM)] * 10,
        out_specs=pl.BlockSpec(memory_space=pltpu.VMEM),
        scratch_shapes=[
            pltpu.VMEM((count, NT), jnp.bfloat16),
            pltpu.VMEM((1, count), jnp.int32),
            pltpu.VMEM((1, count), jnp.int32),
            pltpu.VMEM((NT, 4 * NF), jnp.bfloat16),
            pltpu.VMEM((2 * BINS, columns), jnp.bfloat16),
            pltpu.VMEM((4 * NF, columns), jnp.bfloat16),
            pltpu.VMEM((WIN, P_SIZE, slabs), jnp.float32),
            pltpu.VMEM((WIN, 2, slabs), jnp.int32),
            pltpu.VMEM((WIN, 2, P_SIZE, depth), jnp.float32),
            pltpu.VMEM((WIN, 2, P_SIZE, depth), jnp.float32),
            pltpu.VMEM((slabs, 2 * STEPS, LANES), jnp.float32),
            pltpu.VMEM((slabs, 2 * STEPS, LANES), jnp.bfloat16),
            pltpu.VMEM((slabs, 2 * STEPS, LANES), jnp.bfloat16),
            pltpu.VMEM((WIN, 2 * STEPS, LANES), jnp.bfloat16),
            pltpu.VMEM((WIN, columns, depth), jnp.bfloat16),
            pltpu.VMEM((WIN, XW, columns), jnp.bfloat16),
            pltpu.VMEM((WIN, XW, LANES), jnp.float32),
            pltpu.VMEM((WIN, XW, LANES), jnp.float32),
            pltpu.SemaphoreType.DMA((10,)),
            pltpu.SemaphoreType.DMA,
            pltpu.SemaphoreType.DMA,
            pltpu.SemaphoreType.DMA((WIN,)),
            pltpu.SemaphoreType.DMA((WIN,)),
            pltpu.SemaphoreType.DMA((WIN,)),
            pltpu.SemaphoreType.DMA((WIN,)),
        ],
        compiler_params=pltpu.CompilerParams(
            collective_id=0, has_side_effects=True, vmem_limit_bytes=63 * 1024 * 1024
        ),
    )(
        traces,
        centre_ids.reshape(1, count),
        midpoint_bins,
        jnp.asarray(dft_halves()),
        jnp.asarray(slant_halves()),
        jnp.asarray(spread_table()),
        ray_times,
        ray_amps,
        beam_lateral.transpose(0, 2, 3, 1),
        footprint.transpose(1, 2, 0),
    )
    if lax.axis_size("offset") == 1:
        return partial_image
    return lax.psum_scatter(partial_image, "offset", scatter_dimension=0, tiled=True)


def solution(mesh):
    return jax.shard_map(
        shards,
        mesh=mesh,
        in_specs=(
            P("offset", "slab", None),
            P("offset", "slab", None),
            P("offset", "slab"),
            P("offset", "slab", None, None, None),
            P("offset", "slab", None, None, None),
            P("offset", None, None, None),
            P(),
        ),
        out_specs=P("offset", "slab"),
        check_vma=False,
    )
```

```python
import functools
import math

import jax
import jax.numpy as jnp
import ml_dtypes
import numpy as np
from jax import lax
from jax.experimental import pallas as pl
from jax.experimental.pallas import tpu as pltpu
from jax.sharding import PartitionSpec as P

NT = 256
NF = 64
KLO = 8
P_SIZE = 16
BINS = 16
WIN = 7
XW = 128
HALF = (WIN - 1) // 2
STEPS = NF // KLO
LANES = KLO * P_SIZE

slow_step = 0.25
width_scale = 200.0

ORDER = (3, 2, 4, 1, 5, 0, 6)


def halves(table):
    high = table.astype(ml_dtypes.bfloat16)
    low = (table - high.astype(np.float64)).astype(ml_dtypes.bfloat16)
    return high, low


def dft_halves():
    turns = np.outer(np.arange(NT), np.arange(NF) + KLO) % NT * (2.0 * np.pi / NT)
    return np.concatenate(halves(np.concatenate([np.cos(turns), -np.sin(turns)], axis=1)), axis=1)


def by_chunk(table):
    rows = table.shape[0]
    return table.reshape(rows, 2, STEPS, LANES).transpose(2, 1, 0, 3).reshape(-1, rows, LANES)


def slant_halves():
    omega = (np.arange(NF) + KLO) * (2.0 * np.pi / NT)
    slow = (np.arange(P_SIZE) - (P_SIZE - 1) / 2.0) * slow_step
    place = np.arange(BINS) - (BINS - 1) / 2.0
    phase = place[:, None] * (omega[:, None] * slow[None, :]).reshape(1, -1)
    table = by_chunk(np.concatenate([np.cos(phase), np.sin(phase)], axis=1))
    return np.concatenate(halves(table), axis=1)


def spread_table():
    one_of = by_chunk(np.repeat(np.eye(2 * NF), P_SIZE, axis=1))
    return np.concatenate([one_of, one_of], axis=1).astype(ml_dtypes.bfloat16)


def fit_even(values, degree):
    nodes = 0.125 - 0.125 * np.cos((np.arange(400) + 0.5) * np.pi / 400)
    poly = np.polynomial.chebyshev.Chebyshev.fit(nodes, values(np.sqrt(nodes)), degree, domain=[0, 0.25])
    return [float(c) for c in poly.convert(kind=np.polynomial.Polynomial).coef]


COS_FIT = fit_even(lambda y: np.cos(2 * np.pi * y), 7)
SIN_FIT = fit_even(lambda y: np.sin(2 * np.pi * y) / y, 6)


def horner(fit, s):
    total = jnp.full_like(s, fit[-1])
    for c in fit[-2::-1]:
        total = total * s + c
    return total


def turn(y):
    y = y - jnp.floor(y + 0.5)
    s = y * y
    return horner(COS_FIT, s), horner(SIN_FIT, s) * y


def pair(ref, at):
    return jnp.concatenate([ref[at], ref[at + 1]], axis=1)


def kernel(
    slabs, scale,
    traces_in, ids_in, bins_in, dft_in, slant_in, spread_in, times_in, amps_in, lateral_in, footprint_in,
    image,
    traces, ids, bins, dft, slant, spread, lateral, footprint,
    rays, rays_here, sums, send, arrived, beams, u, v, gauss, step,
    load_sem, send_sem, recv_sem, ray_send, ray_recv, beam_send, beam_recv,
):
    me = lax.axis_index("slab")
    parts = image.shape[0] // 128

    def slab_at(k):
        return lax.rem(me + k, slabs)

    loads = [
        pltpu.make_async_copy(source, held, load_sem.at[i])
        for i, (source, held) in enumerate(
            (
                (traces_in.at[0], traces),
                (dft_in, dft),
                (ids_in, ids),
                (bins_in, bins),
                (slant_in, slant),
                (spread_in, spread),
                (times_in.at[0, 0], rays.at[:, 0]),
                (amps_in.at[0, 0], rays.at[:, 1]),
                (lateral_in.at[0], lateral),
                (footprint_in, footprint),
            )
        )
    ]
    for load in loads:
        load.start()

    barrier = pltpu.get_barrier_semaphore()

    def greet(k, carry):
        pl.semaphore_signal(barrier, inc=1, device_id={"slab": slab_at(k)}, device_id_type=pl.DeviceIdType.MESH)
        return carry

    lax.fori_loop(1, slabs, greet, 0)

    def block_copies(first, count):
        return pltpu.make_async_remote_copy(
            src_ref=send.at[pl.ds(slab_at(first), count)] if count == 1 else send.at[pl.ds(0, count)],
            dst_ref=arrived.at[pl.ds(first, count)],
            send_sem=send_sem,
            recv_sem=recv_sem,
            device_id={"slab": slab_at(first)},
            device_id_type=pl.DeviceIdType.MESH,
        )

    def start_block(k, carry):
        block_copies(k, 1).start()
        return carry

    def ray_copy(w):
        return pltpu.make_async_remote_copy(
            src_ref=rays.at[w],
            dst_ref=rays_here.at[w],
            send_sem=ray_send.at[w],
            recv_sem=ray_recv.at[w],
            device_id={"slab": slab_at(slabs + w - HALF)},
            device_id_type=pl.DeviceIdType.MESH,
        )

    def beam_copy(w):
        return pltpu.make_async_remote_copy(
            src_ref=beams.at[HALF],
            dst_ref=beams.at[w],
            send_sem=beam_send.at[w],
            recv_sem=beam_recv.at[w],
            device_id={"slab": slab_at(slabs + w - HALF)},
            device_id_type=pl.DeviceIdType.MESH,
        )

    def goes(w):
        target = me + (w - HALF)
        return (target >= 0) & (target < slabs)

    def comes(w):
        source = me - (w - HALF)
        return (source >= 0) & (source < slabs)

    for load in loads[:4]:
        load.wait()
    spectrum = jnp.dot(traces[...], dft[...], preferred_element_type=jnp.float32)
    spectrum = spectrum[:, : 2 * NF] + spectrum[:, 2 * NF :]
    spec_high = spectrum.astype(jnp.bfloat16)
    spec_low = (spectrum - spec_high.astype(jnp.float32)).astype(jnp.bfloat16)
    spec = jnp.concatenate([spec_high, spec_low], axis=1)
    count = spec.shape[0]
    bin_row = lax.broadcasted_iota(jnp.int32, (2 * BINS, count), 0) % BINS
    bin_hot = jnp.where(bin_row == bins[...], 1.0, 0.0).T.astype(jnp.bfloat16)
    id_row = lax.broadcasted_iota(jnp.int32, (slabs, count), 0)
    id_hot = jnp.where(id_row == ids[...], 1.0, 0.0).astype(jnp.bfloat16)
    id_hot = jnp.concatenate([id_hot, id_hot], axis=1)
    for load in loads[4:8]:
        load.wait()

    pl.semaphore_wait(barrier, slabs - 1)
    for w in ORDER[1:]:

        @pl.when(goes(w))
        def _():
            ray_copy(w).start()

        @pl.when(jnp.logical_not(comes(w)))
        def _():
            rays_here[w] = rays[w]
            beams[w] = jnp.zeros_like(beams[w])

    for chunk in range(STEPS):
        spec_wide = jnp.dot(spec, pair(spread, 2 * chunk), preferred_element_type=jnp.float32)
        turn_wide = jnp.dot(bin_hot, pair(slant, 2 * chunk), preferred_element_type=jnp.float32)
        spec_re, spec_im = spec_wide[:, :LANES], spec_wide[:, LANES:]
        cosine, sine = turn_wide[:, :LANES], turn_wide[:, LANES:]
        terms = jnp.concatenate(
            [spec_re * cosine + spec_im * sine, spec_im * cosine - spec_re * sine], axis=1
        )
        high = terms.astype(jnp.bfloat16)
        low = (terms - high.astype(jnp.float32)).astype(jnp.bfloat16)
        partial = jnp.dot(
            id_hot, jnp.concatenate([high, low], axis=0), preferred_element_type=jnp.float32
        )
        sums[:, 2 * chunk, :] = partial[:, :LANES] * scale
        sums[:, 2 * chunk + 1, :] = partial[:, LANES:] * scale
    send[...] = sums[...].astype(jnp.bfloat16)
    lax.fori_loop(1, slabs, start_block, 0)

    def make_u(w, held):
        for part in range(parts):
            z = slice(part * 128, (part + 1) * 128)
            make_u_part(w, part, held[w, 0, :, z], held[w, 1, :, z])

    def make_u_part(w, part, t, a):
        cos8, sin8 = turn(t * (KLO / NT))
        cos1, sin1 = turn(t * (1.0 / NT))
        twice = 2.0 * cos8
        re, im = a, jnp.zeros_like(a)
        for b in range(KLO):
            if b:
                re, im = re * cos1 + im * sin1, im * cos1 - re * sin1
            last_re, last_im = re, im
            now_re, now_im = re * cos8 + im * sin8, im * cos8 - re * sin8
            for chunk in range(STEPS):
                at = 2 * chunk * LANES + b * P_SIZE
                u[w, part, at : at + P_SIZE, :] = now_re.astype(jnp.bfloat16)
                u[w, part, at + LANES : at + LANES + P_SIZE, :] = now_im.astype(jnp.bfloat16)
                if chunk < STEPS - 1:
                    now_re, last_re = twice * now_re - last_re, now_re
                    now_im, last_im = twice * now_im - last_im, now_im

    lane = lax.broadcasted_iota(jnp.int32, (1, LANES), 1)
    place = lax.broadcasted_iota(jnp.int32, (XW, LANES), 0).astype(jnp.float32)
    slow_row = lax.broadcasted_iota(jnp.int32, (P_SIZE, LANES), 0)
    slow_lane = lax.broadcasted_iota(jnp.int32, (P_SIZE, LANES), 1) % P_SIZE
    rate = -2.0 * math.pi / NT / width_scale * math.log2(math.e)
    rates = (lane // P_SIZE + KLO).astype(jnp.float32) * rate

    def pick(values, w):
        centre = jnp.clip(me - (w - HALF), 0, slabs - 1)
        held = lax.broadcasted_iota(jnp.int32, values.shape, 1) == centre
        return jnp.sum(jnp.where(held, values, 0.0), axis=1, keepdims=True)

    def make_gauss(w):
        axis = pick(lateral[w], w)
        axis = jnp.sum(jnp.where(slow_row == slow_lane, axis, 0.0), axis=0, keepdims=True)
        ends = pick(footprint[w].astype(jnp.float32), w)
        off = place - axis
        off = jnp.where((place >= ends[0:1]) & (place < ends[1:2]), off * off, 1e9)
        gauss[w] = jnp.exp2(off * rates) * (1.0 / math.sqrt(P_SIZE * NF))
        step[w] = jnp.exp2(off * (KLO * rate))

    def slot_image(w):
        here = beams[w].astype(jnp.float32)
        g = gauss[w]
        for chunk in range(STEPS):
            if chunk:
                g = g * step[w]
            for at in (2 * chunk, 2 * chunk + 1):
                v[w, at] = (g * here[at : at + 1]).astype(jnp.bfloat16)
        return jnp.dot(
            jnp.concatenate([v[w, at] for at in range(2 * STEPS)], axis=1),
            jnp.concatenate([u[w, part] for part in range(parts)], axis=1),
            preferred_element_type=jnp.float32,
        )

    def take_rays(w):
        @pl.when(comes(w))
        def _():
            ray_copy(w).wait_recv()

        make_u(w, rays_here)

    make_u(HALF, rays)
    for load in loads[8:]:
        load.wait()
    for w in ORDER:
        make_gauss(w)
    for w in ORDER[1:5]:
        take_rays(w)

    arrived[0] = send[me]
    block_copies(1, slabs - 1).wait_recv()
    own = jnp.sum(arrived[...].astype(jnp.float32), axis=0)
    beams[HALF] = own.astype(jnp.bfloat16)
    for w in ORDER[1:]:

        @pl.when(goes(w))
        def _():
            beam_copy(w).start()

    for w in ORDER[5:]:
        take_rays(w)
    total = slot_image(HALF)
    for w in ORDER[1:]:

        @pl.when(comes(w))
        def _():
            beam_copy(w).wait_recv()

    for w in ORDER[1:]:
        total += slot_image(w)
    image[...] = total.T

    block_copies(1, slabs - 1).wait_send()
    for w in ORDER[1:]:

        @pl.when(goes(w))
        def _():
            ray_copy(w).wait_send()
            beam_copy(w).wait_send()


def shards(traces, centre_ids, midpoint_bins, ray_times, ray_amps, beam_lateral, footprint):
    slabs = lax.axis_size("slab")
    count = traces.shape[1]
    depth = ray_times.shape[4]
    columns = 2 * NF * P_SIZE
    operands = (
        traces,
        centre_ids.reshape(1, count),
        midpoint_bins,
        jnp.asarray(dft_halves()),
        jnp.asarray(slant_halves()),
        jnp.asarray(spread_table()),
        ray_times,
        ray_amps,
        beam_lateral.transpose(0, 2, 3, 1),
        footprint.transpose(1, 2, 0),
    )
    partial_image = pl.pallas_call(
        functools.partial(kernel, slabs, 1.0 / math.sqrt(NT * count)),
        out_shape=jax.ShapeDtypeStruct((depth, XW), jnp.float32),
        in_specs=[pl.BlockSpec(memory_space=pltpu.HBM)] * 10,
        out_specs=pl.BlockSpec(memory_space=pltpu.VMEM),
        scratch_shapes=[
            pltpu.VMEM((count, NT), jnp.bfloat16),
            pltpu.VMEM((1, count), jnp.int32),
            pltpu.VMEM((1, count), jnp.int32),
            pltpu.VMEM((NT, 4 * NF), jnp.bfloat16),
            pltpu.VMEM((2 * STEPS, 2 * BINS, LANES), jnp.bfloat16),
            pltpu.VMEM((2 * STEPS, 4 * NF, LANES), jnp.bfloat16),
            pltpu.VMEM((WIN, P_SIZE, slabs), jnp.float32),
            pltpu.VMEM((WIN, 2, slabs), jnp.int32),
            pltpu.VMEM((WIN, 2, P_SIZE, depth), jnp.float32),
            pltpu.VMEM((WIN, 2, P_SIZE, depth), jnp.float32),
            pltpu.VMEM((slabs, 2 * STEPS, LANES), jnp.float32),
            pltpu.VMEM((slabs, 2 * STEPS, LANES), jnp.bfloat16),
            pltpu.VMEM((slabs, 2 * STEPS, LANES), jnp.bfloat16),
            pltpu.VMEM((WIN, 2 * STEPS, LANES), jnp.bfloat16),
            pltpu.VMEM((WIN, depth // 128, columns, 128), jnp.bfloat16),
            pltpu.VMEM((WIN, 2 * STEPS, XW, LANES), jnp.bfloat16),
            pltpu.VMEM((WIN, XW, LANES), jnp.float32),
            pltpu.VMEM((WIN, XW, LANES), jnp.float32),
            pltpu.SemaphoreType.DMA((10,)),
            pltpu.SemaphoreType.DMA,
            pltpu.SemaphoreType.DMA,
            pltpu.SemaphoreType.DMA((WIN,)),
            pltpu.SemaphoreType.DMA((WIN,)),
            pltpu.SemaphoreType.DMA((WIN,)),
            pltpu.SemaphoreType.DMA((WIN,)),
        ],
        compiler_params=pltpu.CompilerParams(
            collective_id=0, has_side_effects=True, vmem_limit_bytes=40 * 1024 * 1024
        ),
    )(*[pltpu.with_memory_space_constraint(operand, pltpu.HBM) for operand in operands])
    if lax.axis_size("offset") == 1:
        return partial_image
    return lax.psum_scatter(partial_image, "offset", scatter_dimension=0, tiled=True)


def solution(mesh):
    return jax.shard_map(
        shards,
        mesh=mesh,
        in_specs=(
            P("offset", "slab", None),
            P("offset", "slab", None),
            P("offset", "slab"),
            P("offset", "slab", None, None, None),
            P("offset", "slab", None, None, None),
            P("offset", None, None, None),
            P(),
        ),
        out_specs=P("offset", "slab"),
        check_vma=False,
    )
```

```python
import functools
import math

import jax
import jax.numpy as jnp
import ml_dtypes
import numpy as np
from jax import lax
from jax.experimental import pallas as pl
from jax.experimental.pallas import tpu as pltpu
from jax.sharding import PartitionSpec as P

NT = 256
NF = 64
KLO = 8
P_SIZE = 16
BINS = 16
WIN = 7
XW = 128
HALF = (WIN - 1) // 2
STEPS = NF // KLO
LANES = KLO * P_SIZE

slow_step = 0.25
width_scale = 200.0

def order(i):
    return HALF + (i + 1) // 2 * (1 - 2 * (i % 2))


OTHERS = [order(i) for i in range(1, WIN)]


def halves(table):
    high = table.astype(ml_dtypes.bfloat16)
    low = (table - high.astype(np.float64)).astype(ml_dtypes.bfloat16)
    return high, low


def dft_halves():
    turns = np.outer(np.arange(NT), np.arange(NF) + KLO) % NT * (2.0 * np.pi / NT)
    return np.concatenate(halves(np.concatenate([np.cos(turns), -np.sin(turns)], axis=1)), axis=1)


def by_chunk(table):
    rows = table.shape[0]
    return table.reshape(rows, 2, STEPS, LANES).transpose(2, 1, 0, 3).reshape(-1, rows, LANES)


def slant_halves():
    omega = (np.arange(NF) + KLO) * (2.0 * np.pi / NT)
    slow = (np.arange(P_SIZE) - (P_SIZE - 1) / 2.0) * slow_step
    place = np.arange(BINS) - (BINS - 1) / 2.0
    phase = place[:, None] * (omega[:, None] * slow[None, :]).reshape(1, -1)
    table = by_chunk(np.concatenate([np.cos(phase), np.sin(phase)], axis=1))
    return np.concatenate(halves(table), axis=1)


def spread_table():
    one_of = by_chunk(np.repeat(np.eye(2 * NF), P_SIZE, axis=1))
    return np.concatenate([one_of, one_of], axis=1).astype(ml_dtypes.bfloat16)


def fit_even(values, degree):
    nodes = 0.125 - 0.125 * np.cos((np.arange(400) + 0.5) * np.pi / 400)
    poly = np.polynomial.chebyshev.Chebyshev.fit(nodes, values(np.sqrt(nodes)), degree, domain=[0, 0.25])
    return [float(c) for c in poly.convert(kind=np.polynomial.Polynomial).coef]


COS_FIT = fit_even(lambda y: np.cos(2 * np.pi * y), 7)
SIN_FIT = fit_even(lambda y: np.sin(2 * np.pi * y) / y, 6)


def horner(fit, s):
    total = jnp.full_like(s, fit[-1])
    for c in fit[-2::-1]:
        total = total * s + c
    return total


def turn(y):
    y = y - jnp.floor(y + 0.5)
    s = y * y
    return horner(COS_FIT, s), horner(SIN_FIT, s) * y


def pair(ref, at):
    return jnp.concatenate([ref[at], ref[at + 1]], axis=1)


def kernel(
    slabs, scale,
    traces_in, ids_in, bins_in, dft_in, slant_in, spread_in, times_in, amps_in, lateral_in, footprint_in,
    image,
    traces, ids, bins, dft, slant, spread, lateral, footprint,
    rays, rays_here, sums, send, arrived, beams, u, v, gauss, step, total,
    load_sem, send_sem, recv_sem, ray_send, ray_recv, beam_send, beam_recv,
):
    me = lax.axis_index("slab")
    parts = image.shape[0] // 128

    def slab_at(k):
        return lax.rem(me + k, slabs)

    loads = [
        pltpu.make_async_copy(source, held, load_sem.at[i])
        for i, (source, held) in enumerate(
            (
                (traces_in.at[0], traces),
                (dft_in, dft),
                (ids_in, ids),
                (bins_in, bins),
                (slant_in, slant),
                (spread_in, spread),
                (times_in.at[0, 0], rays.at[:, 0]),
                (amps_in.at[0, 0], rays.at[:, 1]),
                (lateral_in.at[0], lateral),
                (footprint_in, footprint),
            )
        )
    ]
    for load in loads:
        load.start()

    barrier = pltpu.get_barrier_semaphore()

    def greet(k, carry):
        pl.semaphore_signal(barrier, inc=1, device_id={"slab": slab_at(k)}, device_id_type=pl.DeviceIdType.MESH)
        return carry

    lax.fori_loop(1, slabs, greet, 0)

    def block_copies(first, count):
        return pltpu.make_async_remote_copy(
            src_ref=send.at[pl.ds(slab_at(first), count)] if count == 1 else send.at[pl.ds(0, count)],
            dst_ref=arrived.at[pl.ds(first, count)],
            send_sem=send_sem,
            recv_sem=recv_sem,
            device_id={"slab": slab_at(first)},
            device_id_type=pl.DeviceIdType.MESH,
        )

    def start_block(k, carry):
        block_copies(k, 1).start()
        return carry

    def ray_copy(w):
        return pltpu.make_async_remote_copy(
            src_ref=rays.at[w],
            dst_ref=rays_here.at[w],
            send_sem=ray_send.at[w],
            recv_sem=ray_recv.at[w],
            device_id={"slab": slab_at(slabs + w - HALF)},
            device_id_type=pl.DeviceIdType.MESH,
        )

    def beam_copy(w):
        return pltpu.make_async_remote_copy(
            src_ref=beams.at[HALF],
            dst_ref=beams.at[w],
            send_sem=beam_send.at[w],
            recv_sem=beam_recv.at[w],
            device_id={"slab": slab_at(slabs + w - HALF)},
            device_id_type=pl.DeviceIdType.MESH,
        )

    def goes(w):
        target = me + (w - HALF)
        return (target >= 0) & (target < slabs)

    def comes(w):
        source = me - (w - HALF)
        return (source >= 0) & (source < slabs)

    for load in loads[:4]:
        load.wait()
    spectrum = jnp.dot(traces[...], dft[...], preferred_element_type=jnp.float32)
    spectrum = spectrum[:, : 2 * NF] + spectrum[:, 2 * NF :]
    spec_high = spectrum.astype(jnp.bfloat16)
    spec_low = (spectrum - spec_high.astype(jnp.float32)).astype(jnp.bfloat16)
    spec = jnp.concatenate([spec_high, spec_low], axis=1)
    count = spec.shape[0]
    bin_row = lax.broadcasted_iota(jnp.int32, (2 * BINS, count), 0) % BINS
    bin_hot = jnp.where(bin_row == bins[...], 1.0, 0.0).T.astype(jnp.bfloat16)
    id_row = lax.broadcasted_iota(jnp.int32, (slabs, count), 0)
    id_hot = jnp.where(id_row == ids[...], 1.0, 0.0).astype(jnp.bfloat16)
    id_hot = jnp.concatenate([id_hot, id_hot], axis=1)
    for load in loads[4:8]:
        load.wait()

    pl.semaphore_wait(barrier, slabs - 1)
    for w in OTHERS:

        @pl.when(goes(w))
        def _():
            ray_copy(w).start()

        @pl.when(jnp.logical_not(comes(w)))
        def _():
            rays_here[w] = rays[w]
            beams[w] = jnp.zeros_like(beams[w])

    for chunk in range(STEPS):
        spec_wide = jnp.dot(spec, pair(spread, 2 * chunk), preferred_element_type=jnp.float32)
        turn_wide = jnp.dot(bin_hot, pair(slant, 2 * chunk), preferred_element_type=jnp.float32)
        spec_re, spec_im = spec_wide[:, :LANES], spec_wide[:, LANES:]
        cosine, sine = turn_wide[:, :LANES], turn_wide[:, LANES:]
        terms = jnp.concatenate(
            [spec_re * cosine + spec_im * sine, spec_im * cosine - spec_re * sine], axis=1
        )
        high = terms.astype(jnp.bfloat16)
        low = (terms - high.astype(jnp.float32)).astype(jnp.bfloat16)
        partial = jnp.dot(
            id_hot, jnp.concatenate([high, low], axis=0), preferred_element_type=jnp.float32
        )
        sums[:, 2 * chunk, :] = partial[:, :LANES] * scale
        sums[:, 2 * chunk + 1, :] = partial[:, LANES:] * scale
    send[...] = sums[...].astype(jnp.bfloat16)
    lax.fori_loop(1, slabs, start_block, 0)

    def make_u(w, held):
        for part in range(parts):
            z = slice(part * 128, (part + 1) * 128)
            make_u_part(w, part, held[w, 0, :, z], held[w, 1, :, z])

    def make_u_part(w, part, t, a):
        cos8, sin8 = turn(t * (KLO / NT))
        cos1, sin1 = turn(t * (1.0 / NT))
        twice = 2.0 * cos8
        re, im = a, jnp.zeros_like(a)
        for b in range(KLO):
            if b:
                re, im = re * cos1 + im * sin1, im * cos1 - re * sin1
            last_re, last_im = re, im
            now_re, now_im = re * cos8 + im * sin8, im * cos8 - re * sin8
            for chunk in range(STEPS):
                at = 2 * chunk * LANES + b * P_SIZE
                u[w, part, at : at + P_SIZE, :] = now_re.astype(jnp.bfloat16)
                u[w, part, at + LANES : at + LANES + P_SIZE, :] = now_im.astype(jnp.bfloat16)
                if chunk < STEPS - 1:
                    now_re, last_re = twice * now_re - last_re, now_re
                    now_im, last_im = twice * now_im - last_im, now_im

    lane = lax.broadcasted_iota(jnp.int32, (1, LANES), 1)
    place = lax.broadcasted_iota(jnp.int32, (XW, LANES), 0).astype(jnp.float32)
    slow_row = lax.broadcasted_iota(jnp.int32, (P_SIZE, LANES), 0)
    slow_lane = lax.broadcasted_iota(jnp.int32, (P_SIZE, LANES), 1) % P_SIZE
    rate = -2.0 * math.pi / NT / width_scale * math.log2(math.e)
    rates = (lane // P_SIZE + KLO).astype(jnp.float32) * rate

    def pick(values, w):
        centre = jnp.clip(me - (w - HALF), 0, slabs - 1)
        held = lax.broadcasted_iota(jnp.int32, values.shape, 1) == centre
        return jnp.sum(jnp.where(held, values, 0.0), axis=1, keepdims=True)

    def make_gauss(w, carry):
        axis = pick(lateral[w], w)
        axis = jnp.sum(jnp.where(slow_row == slow_lane, axis, 0.0), axis=0, keepdims=True)
        ends = pick(footprint[w].astype(jnp.float32), w)
        off = place - axis
        off = jnp.where((place >= ends[0:1]) & (place < ends[1:2]), off * off, 1e9)
        gauss[w] = jnp.exp2(off * rates) * (1.0 / math.sqrt(P_SIZE * NF))
        step[w] = jnp.exp2(off * (KLO * rate))
        return carry

    def slot_image(w):
        here = beams[w].astype(jnp.float32)
        g = gauss[w]
        for chunk in range(STEPS):
            if chunk:
                g = g * step[w]
            for at in (2 * chunk, 2 * chunk + 1):
                v[w, at] = (g * here[at : at + 1]).astype(jnp.bfloat16)
        return jnp.dot(
            jnp.concatenate([v[w, at] for at in range(2 * STEPS)], axis=1),
            jnp.concatenate([u[w, part] for part in range(parts)], axis=1),
            preferred_element_type=jnp.float32,
        )

    def take_rays(i, carry):
        w = order(i)

        @pl.when(comes(w) & (w != HALF))
        def _():
            ray_copy(w).wait_recv()

        make_u(w, rays_here)
        return carry

    rays_here[HALF] = rays[HALF]
    for load in loads[8:]:
        load.wait()
    lax.fori_loop(0, WIN, make_gauss, 0)
    lax.fori_loop(0, 5, take_rays, 0)

    arrived[0] = send[me]
    block_copies(1, slabs - 1).wait_recv()
    own = jnp.sum(arrived[...].astype(jnp.float32), axis=0)
    beams[HALF] = own.astype(jnp.bfloat16)
    for w in OTHERS:

        @pl.when(goes(w))
        def _():
            beam_copy(w).start()

    lax.fori_loop(5, WIN, take_rays, 0)
    total[...] = jnp.zeros_like(total)

    def add_slot(i, carry):
        w = order(i)

        @pl.when(comes(w) & (w != HALF))
        def _():
            beam_copy(w).wait_recv()

        total[...] += slot_image(w)
        return carry

    lax.fori_loop(0, WIN, add_slot, 0)
    image[...] = total[...].T

    block_copies(1, slabs - 1).wait_send()
    for w in OTHERS:

        @pl.when(goes(w))
        def _():
            ray_copy(w).wait_send()
            beam_copy(w).wait_send()


def shards(traces, centre_ids, midpoint_bins, ray_times, ray_amps, beam_lateral, footprint):
    slabs = lax.axis_size("slab")
    count = traces.shape[1]
    depth = ray_times.shape[4]
    columns = 2 * NF * P_SIZE
    operands = (
        traces,
        centre_ids.reshape(1, count),
        midpoint_bins,
        jnp.asarray(dft_halves()),
        jnp.asarray(slant_halves()),
        jnp.asarray(spread_table()),
        ray_times,
        ray_amps,
        beam_lateral.transpose(0, 2, 3, 1),
        footprint.transpose(1, 2, 0),
    )
    partial_image = pl.pallas_call(
        functools.partial(kernel, slabs, 1.0 / math.sqrt(NT * count)),
        out_shape=jax.ShapeDtypeStruct((depth, XW), jnp.float32),
        in_specs=[pl.BlockSpec(memory_space=pltpu.HBM)] * 10,
        out_specs=pl.BlockSpec(memory_space=pltpu.VMEM),
        scratch_shapes=[
            pltpu.VMEM((count, NT), jnp.bfloat16),
            pltpu.VMEM((1, count), jnp.int32),
            pltpu.VMEM((1, count), jnp.int32),
            pltpu.VMEM((NT, 4 * NF), jnp.bfloat16),
            pltpu.VMEM((2 * STEPS, 2 * BINS, LANES), jnp.bfloat16),
            pltpu.VMEM((2 * STEPS, 4 * NF, LANES), jnp.bfloat16),
            pltpu.VMEM((WIN, P_SIZE, slabs), jnp.float32),
            pltpu.VMEM((WIN, 2, slabs), jnp.int32),
            pltpu.VMEM((WIN, 2, P_SIZE, depth), jnp.float32),
            pltpu.VMEM((WIN, 2, P_SIZE, depth), jnp.float32),
            pltpu.VMEM((slabs, 2 * STEPS, LANES), jnp.float32),
            pltpu.VMEM((slabs, 2 * STEPS, LANES), jnp.bfloat16),
            pltpu.VMEM((slabs, 2 * STEPS, LANES), jnp.bfloat16),
            pltpu.VMEM((WIN, 2 * STEPS, LANES), jnp.bfloat16),
            pltpu.VMEM((WIN, depth // 128, columns, 128), jnp.bfloat16),
            pltpu.VMEM((WIN, 2 * STEPS, XW, LANES), jnp.bfloat16),
            pltpu.VMEM((WIN, XW, LANES), jnp.float32),
            pltpu.VMEM((WIN, XW, LANES), jnp.float32),
            pltpu.VMEM((XW, depth), jnp.float32),
            pltpu.SemaphoreType.DMA((10,)),
            pltpu.SemaphoreType.DMA,
            pltpu.SemaphoreType.DMA,
            pltpu.SemaphoreType.DMA((WIN,)),
            pltpu.SemaphoreType.DMA((WIN,)),
            pltpu.SemaphoreType.DMA((WIN,)),
            pltpu.SemaphoreType.DMA((WIN,)),
        ],
        compiler_params=pltpu.CompilerParams(
            collective_id=0, has_side_effects=True, vmem_limit_bytes=40 * 1024 * 1024
        ),
    )(*[pltpu.with_memory_space_constraint(operand, pltpu.HBM) for operand in operands])
    if lax.axis_size("offset") == 1:
        return partial_image
    return lax.psum_scatter(partial_image, "offset", scatter_dimension=0, tiled=True)


def solution(mesh):
    return jax.shard_map(
        shards,
        mesh=mesh,
        in_specs=(
            P("offset", "slab", None),
            P("offset", "slab", None),
            P("offset", "slab"),
            P("offset", "slab", None, None, None),
            P("offset", "slab", None, None, None),
            P("offset", None, None, None),
            P(),
        ),
        out_specs=P("offset", "slab"),
        check_vma=False,
    )
```

```python
import functools
import math

import jax
import jax.numpy as jnp
import ml_dtypes
import numpy as np
from jax import lax
from jax.experimental import pallas as pl
from jax.experimental.pallas import tpu as pltpu
from jax.sharding import PartitionSpec as P

NT = 256
NF = 64
KLO = 8
P_SIZE = 16
BINS = 16
WIN = 7
XW = 128
HALF = (WIN - 1) // 2
STEPS = NF // KLO
LANES = KLO * P_SIZE

slow_step = 0.25
width_scale = 200.0

def order(i):
    return HALF + (i + 1) // 2 * (1 - 2 * (i % 2))


OTHERS = [order(i) for i in range(1, WIN)]


def halves(table):
    high = table.astype(ml_dtypes.bfloat16)
    low = (table - high.astype(np.float64)).astype(ml_dtypes.bfloat16)
    return high, low


def dft_halves():
    turns = np.outer(np.arange(NF) + KLO, np.arange(NT)) % NT * (2.0 * np.pi / NT)
    table = np.stack([np.cos(turns), -np.sin(turns)]).reshape(2, STEPS, KLO, NT)
    return np.concatenate(halves(table.transpose(1, 0, 2, 3).reshape(2 * NF, NT)), axis=0)


def by_chunk(table):
    rows = table.shape[0]
    return table.reshape(rows, 2, STEPS, LANES).transpose(2, 1, 0, 3).reshape(-1, rows, LANES)


def slant_halves():
    omega = (np.arange(NF) + KLO) * (2.0 * np.pi / NT)
    slow = (np.arange(P_SIZE) - (P_SIZE - 1) / 2.0) * slow_step
    place = np.arange(BINS) - (BINS - 1) / 2.0
    phase = place[:, None] * (omega[:, None] * slow[None, :]).reshape(1, -1)
    table = by_chunk(np.concatenate([np.cos(phase), np.sin(phase)], axis=1))
    return np.concatenate(halves(table), axis=1)


def spread_table():
    one_of = np.repeat(np.eye(2 * KLO), P_SIZE, axis=1).reshape(2 * KLO, 2, LANES).transpose(1, 0, 2)
    return np.concatenate([one_of, one_of], axis=1).astype(ml_dtypes.bfloat16)


def fit_even(values, degree):
    nodes = 0.125 - 0.125 * np.cos((np.arange(400) + 0.5) * np.pi / 400)
    poly = np.polynomial.chebyshev.Chebyshev.fit(nodes, values(np.sqrt(nodes)), degree, domain=[0, 0.25])
    return [float(c) for c in poly.convert(kind=np.polynomial.Polynomial).coef]


COS_FIT = fit_even(lambda y: np.cos(2 * np.pi * y), 7)
SIN_FIT = fit_even(lambda y: np.sin(2 * np.pi * y) / y, 6)


def horner(fit, s):
    total = jnp.full_like(s, fit[-1])
    for c in fit[-2::-1]:
        total = total * s + c
    return total


def turn(y):
    y = y - jnp.floor(y + 0.5)
    s = y * y
    return horner(COS_FIT, s), horner(SIN_FIT, s) * y


def pair(ref, at):
    return jnp.concatenate([ref[at], ref[at + 1]], axis=1)


def kernel(
    slabs, scale,
    traces_in, ids_in, bins_in, dft_in, slant_in, spread_in, times_in, amps_in, lateral_in, footprint_in,
    image,
    traces, ids, bins, dft, slant, spread, lateral, footprint,
    rays, rays_here, sums, send, arrived, beams, u, v, gauss, step, total,
    load_sem, send_sem, recv_sem, ray_send, ray_recv, beam_send, beam_recv,
):
    me = lax.axis_index("slab")
    parts = image.shape[0] // 128

    def slab_at(k):
        return lax.rem(me + k, slabs)

    loads = [
        pltpu.make_async_copy(source, held, load_sem.at[i])
        for i, (source, held) in enumerate(
            (
                (traces_in.at[0], traces),
                (dft_in, dft),
                (ids_in, ids),
                (bins_in, bins),
                (slant_in, slant),
                (spread_in, spread),
                (times_in.at[0, 0], rays.at[:, 0]),
                (amps_in.at[0, 0], rays.at[:, 1]),
                (lateral_in.at[0], lateral),
                (footprint_in, footprint),
            )
        )
    ]
    for load in loads:
        load.start()

    barrier = pltpu.get_barrier_semaphore()

    def greet(k, carry):
        pl.semaphore_signal(barrier, inc=1, device_id={"slab": slab_at(k)}, device_id_type=pl.DeviceIdType.MESH)
        return carry

    lax.fori_loop(1, slabs, greet, 0)

    def block_copies(first, count):
        return pltpu.make_async_remote_copy(
            src_ref=send.at[pl.ds(slab_at(first), count)] if count == 1 else send.at[pl.ds(0, count)],
            dst_ref=arrived.at[pl.ds(first, count)],
            send_sem=send_sem,
            recv_sem=recv_sem,
            device_id={"slab": slab_at(first)},
            device_id_type=pl.DeviceIdType.MESH,
        )

    def start_block(k, carry):
        block_copies(k, 1).start()
        return carry

    def ray_copy(w):
        return pltpu.make_async_remote_copy(
            src_ref=rays.at[w],
            dst_ref=rays_here.at[w],
            send_sem=ray_send.at[w],
            recv_sem=ray_recv.at[w],
            device_id={"slab": slab_at(slabs + w - HALF)},
            device_id_type=pl.DeviceIdType.MESH,
        )

    def beam_copy(w):
        return pltpu.make_async_remote_copy(
            src_ref=beams.at[HALF],
            dst_ref=beams.at[w],
            send_sem=beam_send.at[w],
            recv_sem=beam_recv.at[w],
            device_id={"slab": slab_at(slabs + w - HALF)},
            device_id_type=pl.DeviceIdType.MESH,
        )

    def goes(w):
        target = me + (w - HALF)
        return (target >= 0) & (target < slabs)

    def comes(w):
        source = me - (w - HALF)
        return (source >= 0) & (source < slabs)

    def send_rays(slots):
        for w in slots:

            @pl.when(goes(w))
            def _():
                ray_copy(w).start()

    for load in loads[:4]:
        load.wait()
    spectrum = lax.dot_general(
        dft[...], traces[...], (((1,), (1,)), ((), ())), preferred_element_type=jnp.float32
    )
    spectrum = spectrum[: 2 * NF] + spectrum[2 * NF :]
    spec_high = spectrum.astype(jnp.bfloat16)
    spec_low = (spectrum - spec_high.astype(jnp.float32)).astype(jnp.bfloat16)
    count = spectrum.shape[1]
    bin_row = lax.broadcasted_iota(jnp.int32, (2 * BINS, count), 0) % BINS
    bin_hot = jnp.where(bin_row == bins[...], 1.0, 0.0).T.astype(jnp.bfloat16)
    id_row = lax.broadcasted_iota(jnp.int32, (slabs, count), 0)
    id_hot = jnp.where(id_row == ids[...], 1.0, 0.0).astype(jnp.bfloat16)
    id_hot = jnp.concatenate([id_hot, id_hot], axis=1)
    for load in loads[4:8]:
        load.wait()

    pl.semaphore_wait(barrier, slabs - 1)
    send_rays(OTHERS[:2])
    for w in OTHERS:

        @pl.when(jnp.logical_not(comes(w)))
        def _():
            rays_here[w] = rays[w]
            beams[w] = jnp.zeros_like(beams[w])

    spread_wide = pair(spread, 0)
    for chunk in range(STEPS):
        rows = slice(2 * chunk * KLO, 2 * (chunk + 1) * KLO)
        spec = jnp.concatenate([spec_high[rows], spec_low[rows]], axis=0)
        spec_wide = lax.dot_general(
            spec, spread_wide, (((0,), (0,)), ((), ())), preferred_element_type=jnp.float32
        )
        turn_wide = jnp.dot(bin_hot, pair(slant, 2 * chunk), preferred_element_type=jnp.float32)
        spec_re, spec_im = spec_wide[:, :LANES], spec_wide[:, LANES:]
        cosine, sine = turn_wide[:, :LANES], turn_wide[:, LANES:]
        terms = jnp.concatenate(
            [spec_re * cosine + spec_im * sine, spec_im * cosine - spec_re * sine], axis=1
        )
        high = terms.astype(jnp.bfloat16)
        low = (terms - high.astype(jnp.float32)).astype(jnp.bfloat16)
        partial = jnp.dot(
            id_hot, jnp.concatenate([high, low], axis=0), preferred_element_type=jnp.float32
        )
        sums[:, 2 * chunk, :] = partial[:, :LANES] * scale
        sums[:, 2 * chunk + 1, :] = partial[:, LANES:] * scale
    send[...] = sums[...].astype(jnp.bfloat16)
    lax.fori_loop(1, slabs, start_block, 0)
    send_rays(OTHERS[2:])

    def make_u(w, held):
        for part in range(parts):
            z = slice(part * 128, (part + 1) * 128)
            make_u_part(w, part, held[w, 0, :, z], held[w, 1, :, z])

    def make_u_part(w, part, t, a):
        cos8, sin8 = turn(t * (KLO / NT))
        cos1, sin1 = turn(t * (1.0 / NT))
        twice = 2.0 * cos8
        re, im = a, jnp.zeros_like(a)
        for b in range(KLO):
            if b:
                re, im = re * cos1 + im * sin1, im * cos1 - re * sin1
            last_re, last_im = re, im
            now_re, now_im = re * cos8 + im * sin8, im * cos8 - re * sin8
            for chunk in range(STEPS):
                at = 2 * chunk * LANES + b * P_SIZE
                u[w, part, at : at + P_SIZE, :] = now_re.astype(jnp.bfloat16)
                u[w, part, at + LANES : at + LANES + P_SIZE, :] = now_im.astype(jnp.bfloat16)
                if chunk < STEPS - 1:
                    now_re, last_re = twice * now_re - last_re, now_re
                    now_im, last_im = twice * now_im - last_im, now_im

    lane = lax.broadcasted_iota(jnp.int32, (1, LANES), 1)
    place = lax.broadcasted_iota(jnp.int32, (XW, LANES), 0).astype(jnp.float32)
    slow_row = lax.broadcasted_iota(jnp.int32, (P_SIZE, LANES), 0)
    slow_lane = lax.broadcasted_iota(jnp.int32, (P_SIZE, LANES), 1) % P_SIZE
    rate = -2.0 * math.pi / NT / width_scale * math.log2(math.e)
    rates = (lane // P_SIZE + KLO).astype(jnp.float32) * rate

    def pick(values, w):
        centre = jnp.clip(me - (w - HALF), 0, slabs - 1)
        held = lax.broadcasted_iota(jnp.int32, values.shape, 1) == centre
        return jnp.sum(jnp.where(held, values, 0.0), axis=1, keepdims=True)

    def make_gauss(w, carry):
        axis = pick(lateral[w], w)
        axis = jnp.sum(jnp.where(slow_row == slow_lane, axis, 0.0), axis=0, keepdims=True)
        ends = pick(footprint[w].astype(jnp.float32), w)
        off = place - axis
        off = jnp.where((place >= ends[0:1]) & (place < ends[1:2]), off * off, 1e9)
        gauss[w] = jnp.exp2(off * rates) * (1.0 / math.sqrt(P_SIZE * NF))
        step[w] = jnp.exp2(off * (KLO * rate))
        return carry

    def slot_image(w):
        here = beams[w].astype(jnp.float32)
        g = gauss[w]
        for chunk in range(STEPS):
            if chunk:
                g = g * step[w]
            for at in (2 * chunk, 2 * chunk + 1):
                v[w, at] = (g * here[at : at + 1]).astype(jnp.bfloat16)
        return jnp.dot(
            jnp.concatenate([v[w, at] for at in range(2 * STEPS)], axis=1),
            jnp.concatenate([u[w, part] for part in range(parts)], axis=1),
            preferred_element_type=jnp.float32,
        )

    def take_rays(i, carry):
        w = order(i)

        @pl.when(comes(w) & (w != HALF))
        def _():
            ray_copy(w).wait_recv()

        make_u(w, rays_here)
        return carry

    rays_here[HALF] = rays[HALF]
    for load in loads[8:]:
        load.wait()
    lax.fori_loop(0, WIN, make_gauss, 0)
    lax.fori_loop(0, 5, take_rays, 0)

    arrived[0] = send[me]
    block_copies(1, slabs - 1).wait_recv()
    own = jnp.sum(arrived[...].astype(jnp.float32), axis=0)
    beams[HALF] = own.astype(jnp.bfloat16)
    for w in OTHERS:

        @pl.when(goes(w))
        def _():
            beam_copy(w).start()

    lax.fori_loop(5, WIN, take_rays, 0)
    total[...] = jnp.zeros_like(total)

    def add_slot(i, carry):
        w = order(i)

        @pl.when(comes(w) & (w != HALF))
        def _():
            beam_copy(w).wait_recv()

        total[...] += slot_image(w)
        return carry

    lax.fori_loop(0, WIN, add_slot, 0)
    image[...] = total[...].T

    block_copies(1, slabs - 1).wait_send()
    for w in OTHERS:

        @pl.when(goes(w))
        def _():
            ray_copy(w).wait_send()
            beam_copy(w).wait_send()


def shards(traces, centre_ids, midpoint_bins, ray_times, ray_amps, beam_lateral, footprint):
    slabs = lax.axis_size("slab")
    count = traces.shape[1]
    depth = ray_times.shape[4]
    columns = 2 * NF * P_SIZE
    operands = (
        traces,
        centre_ids.reshape(1, count),
        midpoint_bins,
        jnp.asarray(dft_halves()),
        jnp.asarray(slant_halves()),
        jnp.asarray(spread_table()),
        ray_times,
        ray_amps,
        beam_lateral.transpose(0, 2, 3, 1),
        footprint.transpose(1, 2, 0),
    )
    partial_image = pl.pallas_call(
        functools.partial(kernel, slabs, 1.0 / math.sqrt(NT * count)),
        out_shape=jax.ShapeDtypeStruct((depth, XW), jnp.float32),
        in_specs=[pl.BlockSpec(memory_space=pltpu.HBM)] * 10,
        out_specs=pl.BlockSpec(memory_space=pltpu.VMEM),
        scratch_shapes=[
            pltpu.VMEM((count, NT), jnp.bfloat16),
            pltpu.VMEM((1, count), jnp.int32),
            pltpu.VMEM((1, count), jnp.int32),
            pltpu.VMEM((4 * NF, NT), jnp.bfloat16),
            pltpu.VMEM((2 * STEPS, 2 * BINS, LANES), jnp.bfloat16),
            pltpu.VMEM((2, 4 * KLO, LANES), jnp.bfloat16),
            pltpu.VMEM((WIN, P_SIZE, slabs), jnp.float32),
            pltpu.VMEM((WIN, 2, slabs), jnp.int32),
            pltpu.VMEM((WIN, 2, P_SIZE, depth), jnp.float32),
            pltpu.VMEM((WIN, 2, P_SIZE, depth), jnp.float32),
            pltpu.VMEM((slabs, 2 * STEPS, LANES), jnp.float32),
            pltpu.VMEM((slabs, 2 * STEPS, LANES), jnp.bfloat16),
            pltpu.VMEM((slabs, 2 * STEPS, LANES), jnp.bfloat16),
            pltpu.VMEM((WIN, 2 * STEPS, LANES), jnp.bfloat16),
            pltpu.VMEM((WIN, depth // 128, columns, 128), jnp.bfloat16),
            pltpu.VMEM((WIN, 2 * STEPS, XW, LANES), jnp.bfloat16),
            pltpu.VMEM((WIN, XW, LANES), jnp.float32),
            pltpu.VMEM((WIN, XW, LANES), jnp.float32),
            pltpu.VMEM((XW, depth), jnp.float32),
            pltpu.SemaphoreType.DMA((10,)),
            pltpu.SemaphoreType.DMA,
            pltpu.SemaphoreType.DMA,
            pltpu.SemaphoreType.DMA((WIN,)),
            pltpu.SemaphoreType.DMA((WIN,)),
            pltpu.SemaphoreType.DMA((WIN,)),
            pltpu.SemaphoreType.DMA((WIN,)),
        ],
        compiler_params=pltpu.CompilerParams(
            collective_id=0, has_side_effects=True, vmem_limit_bytes=40 * 1024 * 1024
        ),
    )(*[pltpu.with_memory_space_constraint(operand, pltpu.HBM) for operand in operands])
    if lax.axis_size("offset") == 1:
        return partial_image
    return lax.psum_scatter(partial_image, "offset", scatter_dimension=0, tiled=True)


def solution(mesh):
    return jax.shard_map(
        shards,
        mesh=mesh,
        in_specs=(
            P("offset", "slab", None),
            P("offset", "slab", None),
            P("offset", "slab"),
            P("offset", "slab", None, None, None),
            P("offset", "slab", None, None, None),
            P("offset", None, None, None),
            P(),
        ),
        out_specs=P("offset", "slab"),
        check_vma=False,
    )
```

```python
import functools
import math

import jax
import jax.numpy as jnp
import ml_dtypes
import numpy as np
from jax import lax
from jax.experimental import pallas as pl
from jax.experimental.pallas import tpu as pltpu
from jax.sharding import PartitionSpec as P

NT = 256
NF = 64
KLO = 8
P_SIZE = 16
BINS = 16
WIN = 7
XW = 128
HALF = (WIN - 1) // 2
STEPS = NF // KLO
LANES = KLO * P_SIZE

slow_step = 0.25
width_scale = 200.0

def order(i):
    return HALF + (i + 1) // 2 * (1 - 2 * (i % 2))


OTHERS = [order(i) for i in range(1, WIN)]


def halves(table):
    high = table.astype(ml_dtypes.bfloat16)
    low = (table - high.astype(np.float64)).astype(ml_dtypes.bfloat16)
    return high, low


def dft_halves():
    turns = np.outer(np.arange(NF) + KLO, np.arange(NT)) % NT * (2.0 * np.pi / NT)
    table = np.stack([np.cos(turns), -np.sin(turns)]).reshape(2, STEPS, KLO, NT)
    return np.concatenate(halves(table.transpose(1, 0, 2, 3).reshape(2 * NF, NT)), axis=0)


def by_chunk(table):
    rows = table.shape[0]
    return table.reshape(rows, 2, STEPS, LANES).transpose(2, 1, 0, 3).reshape(-1, rows, LANES)


def slant_halves():
    omega = (np.arange(NF) + KLO) * (2.0 * np.pi / NT)
    slow = (np.arange(P_SIZE) - (P_SIZE - 1) / 2.0) * slow_step
    place = np.arange(BINS) - (BINS - 1) / 2.0
    phase = place[:, None] * (omega[:, None] * slow[None, :]).reshape(1, -1)
    table = by_chunk(np.concatenate([np.cos(phase), np.sin(phase)], axis=1))
    return np.concatenate(halves(table), axis=1)


def spread_table():
    one_of = np.repeat(np.eye(2 * KLO), P_SIZE, axis=1).reshape(2 * KLO, 2, LANES).transpose(1, 0, 2)
    return np.concatenate([one_of, one_of], axis=1).astype(ml_dtypes.bfloat16)


def fit_even(values, degree):
    nodes = 0.125 - 0.125 * np.cos((np.arange(400) + 0.5) * np.pi / 400)
    poly = np.polynomial.chebyshev.Chebyshev.fit(nodes, values(np.sqrt(nodes)), degree, domain=[0, 0.25])
    return [float(c) for c in poly.convert(kind=np.polynomial.Polynomial).coef]


COS_FIT = fit_even(lambda y: np.cos(2 * np.pi * y), 7)
SIN_FIT = fit_even(lambda y: np.sin(2 * np.pi * y) / y, 6)


def horner(fit, s):
    total = jnp.full_like(s, fit[-1])
    for c in fit[-2::-1]:
        total = total * s + c
    return total


def turn(y):
    y = y - jnp.floor(y + 0.5)
    s = y * y
    return horner(COS_FIT, s), horner(SIN_FIT, s) * y


def pair(ref, at):
    return jnp.concatenate([ref[at], ref[at + 1]], axis=1)


def kernel(
    slabs, scale,
    traces_in, ids_in, bins_in, dft_in, slant_in, spread_in, times_in, amps_in, lateral_in, footprint_in,
    u, gauss, step, beams,
    traces, ids, bins, dft, slant, spread, lateral, footprint,
    rays, rays_here, sums, send, arrived,
    load_sem, send_sem, recv_sem, ray_send, ray_recv, beam_send, beam_recv,
):
    me = lax.axis_index("slab")
    parts = u.shape[1]

    def slab_at(k):
        return lax.rem(me + k, slabs)

    loads = [
        pltpu.make_async_copy(source, held, load_sem.at[i])
        for i, (source, held) in enumerate(
            (
                (traces_in.at[0], traces),
                (dft_in, dft),
                (ids_in, ids),
                (bins_in, bins),
                (slant_in, slant),
                (spread_in, spread),
                (times_in.at[0, 0], rays.at[:, 0]),
                (amps_in.at[0, 0], rays.at[:, 1]),
                (lateral_in.at[0], lateral),
                (footprint_in, footprint),
            )
        )
    ]
    for load in loads:
        load.start()

    barrier = pltpu.get_barrier_semaphore()

    def greet(k, carry):
        pl.semaphore_signal(barrier, inc=1, device_id={"slab": slab_at(k)}, device_id_type=pl.DeviceIdType.MESH)
        return carry

    lax.fori_loop(1, slabs, greet, 0)

    def block_copies(first, count):
        return pltpu.make_async_remote_copy(
            src_ref=send.at[pl.ds(slab_at(first), count)] if count == 1 else send.at[pl.ds(0, count)],
            dst_ref=arrived.at[pl.ds(first, count)],
            send_sem=send_sem,
            recv_sem=recv_sem,
            device_id={"slab": slab_at(first)},
            device_id_type=pl.DeviceIdType.MESH,
        )

    def start_block(k, carry):
        block_copies(k, 1).start()
        return carry

    def ray_copy(w):
        return pltpu.make_async_remote_copy(
            src_ref=rays.at[w],
            dst_ref=rays_here.at[w],
            send_sem=ray_send.at[w],
            recv_sem=ray_recv.at[w],
            device_id={"slab": slab_at(slabs + w - HALF)},
            device_id_type=pl.DeviceIdType.MESH,
        )

    def beam_copy(w):
        return pltpu.make_async_remote_copy(
            src_ref=beams.at[HALF],
            dst_ref=beams.at[w],
            send_sem=beam_send.at[w],
            recv_sem=beam_recv.at[w],
            device_id={"slab": slab_at(slabs + w - HALF)},
            device_id_type=pl.DeviceIdType.MESH,
        )

    def goes(w):
        target = me + (w - HALF)
        return (target >= 0) & (target < slabs)

    def comes(w):
        source = me - (w - HALF)
        return (source >= 0) & (source < slabs)

    def send_rays(slots):
        for w in slots:

            @pl.when(goes(w))
            def _():
                ray_copy(w).start()

    for load in loads[:4]:
        load.wait()
    spectrum = lax.dot_general(
        dft[...], traces[...], (((1,), (1,)), ((), ())), preferred_element_type=jnp.float32
    )
    spectrum = spectrum[: 2 * NF] + spectrum[2 * NF :]
    spec_high = spectrum.astype(jnp.bfloat16)
    spec_low = (spectrum - spec_high.astype(jnp.float32)).astype(jnp.bfloat16)
    count = spectrum.shape[1]
    bin_row = lax.broadcasted_iota(jnp.int32, (2 * BINS, count), 0) % BINS
    bin_hot = jnp.where(bin_row == bins[...], 1.0, 0.0).T.astype(jnp.bfloat16)
    id_row = lax.broadcasted_iota(jnp.int32, (slabs, count), 0)
    id_hot = jnp.where(id_row == ids[...], 1.0, 0.0).astype(jnp.bfloat16)
    id_hot = jnp.concatenate([id_hot, id_hot], axis=1)
    for load in loads[4:8]:
        load.wait()

    pl.semaphore_wait(barrier, slabs - 1)
    send_rays(OTHERS)
    for w in OTHERS:

        @pl.when(jnp.logical_not(comes(w)))
        def _():
            rays_here[w] = rays[w]
            beams[w] = jnp.zeros_like(beams[w])

    spread_wide = pair(spread, 0)
    for chunk in range(STEPS):
        rows = slice(2 * chunk * KLO, 2 * (chunk + 1) * KLO)
        spec = jnp.concatenate([spec_high[rows], spec_low[rows]], axis=0)
        spec_wide = lax.dot_general(
            spec, spread_wide, (((0,), (0,)), ((), ())), preferred_element_type=jnp.float32
        )
        turn_wide = jnp.dot(bin_hot, pair(slant, 2 * chunk), preferred_element_type=jnp.float32)
        spec_re, spec_im = spec_wide[:, :LANES], spec_wide[:, LANES:]
        cosine, sine = turn_wide[:, :LANES], turn_wide[:, LANES:]
        terms = jnp.concatenate(
            [spec_re * cosine + spec_im * sine, spec_im * cosine - spec_re * sine], axis=1
        )
        high = terms.astype(jnp.bfloat16)
        low = (terms - high.astype(jnp.float32)).astype(jnp.bfloat16)
        partial = jnp.dot(
            id_hot, jnp.concatenate([high, low], axis=0), preferred_element_type=jnp.float32
        )
        sums[:, 2 * chunk, :] = partial[:, :LANES] * scale
        sums[:, 2 * chunk + 1, :] = partial[:, LANES:] * scale
    send[...] = sums[...].astype(jnp.bfloat16)
    lax.fori_loop(1, slabs, start_block, 0)

    def make_u(w, held):
        for part in range(parts):
            z = slice(part * 128, (part + 1) * 128)
            make_u_part(w, part, held[w, 0, :, z], held[w, 1, :, z])

    def make_u_part(w, part, t, a):
        cos8, sin8 = turn(t * (KLO / NT))
        cos1, sin1 = turn(t * (1.0 / NT))
        twice = 2.0 * cos8
        re, im = a, jnp.zeros_like(a)
        for b in range(KLO):
            if b:
                re, im = re * cos1 + im * sin1, im * cos1 - re * sin1
            last_re, last_im = re, im
            now_re, now_im = re * cos8 + im * sin8, im * cos8 - re * sin8
            for chunk in range(STEPS):
                at = 2 * chunk * LANES + b * P_SIZE
                u[w, part, at : at + P_SIZE, :] = now_re.astype(jnp.bfloat16)
                u[w, part, at + LANES : at + LANES + P_SIZE, :] = now_im.astype(jnp.bfloat16)
                if chunk < STEPS - 1:
                    now_re, last_re = twice * now_re - last_re, now_re
                    now_im, last_im = twice * now_im - last_im, now_im

    lane = lax.broadcasted_iota(jnp.int32, (1, LANES), 1)
    place = lax.broadcasted_iota(jnp.int32, (XW, LANES), 0).astype(jnp.float32)
    slow_row = lax.broadcasted_iota(jnp.int32, (P_SIZE, LANES), 0)
    slow_lane = lax.broadcasted_iota(jnp.int32, (P_SIZE, LANES), 1) % P_SIZE
    rate = -2.0 * math.pi / NT / width_scale * math.log2(math.e)
    rates = (lane // P_SIZE + KLO).astype(jnp.float32) * rate

    def pick(values, w):
        centre = jnp.clip(me - (w - HALF), 0, slabs - 1)
        held = lax.broadcasted_iota(jnp.int32, values.shape, 1) == centre
        return jnp.sum(jnp.where(held, values, 0.0), axis=1, keepdims=True)

    def make_gauss(w, carry):
        axis = pick(lateral[w], w)
        axis = jnp.sum(jnp.where(slow_row == slow_lane, axis, 0.0), axis=0, keepdims=True)
        ends = pick(footprint[w].astype(jnp.float32), w)
        off = place - axis
        off = jnp.where((place >= ends[0:1]) & (place < ends[1:2]), off * off, 1e9)
        gauss[w] = jnp.exp2(off * rates) * (1.0 / math.sqrt(P_SIZE * NF))
        step[w] = jnp.exp2(off * (KLO * rate))
        return carry

    def take_rays(i, carry):
        w = order(i)

        @pl.when(comes(w) & (w != HALF))
        def _():
            ray_copy(w).wait_recv()

        make_u(w, rays_here)
        return carry

    rays_here[HALF] = rays[HALF]
    for load in loads[8:]:
        load.wait()
    lax.fori_loop(0, WIN, make_gauss, 0)
    lax.fori_loop(0, 5, take_rays, 0)

    arrived[0] = send[me]
    block_copies(1, slabs - 1).wait_recv()
    own = jnp.sum(arrived[...].astype(jnp.float32), axis=0)
    beams[HALF] = own.astype(jnp.bfloat16)
    for w in OTHERS:

        @pl.when(goes(w))
        def _():
            beam_copy(w).start()

    lax.fori_loop(5, WIN, take_rays, 0)
    for w in OTHERS:

        @pl.when(comes(w))
        def _():
            beam_copy(w).wait_recv()

    block_copies(1, slabs - 1).wait_send()
    for w in OTHERS:

        @pl.when(goes(w))
        def _():
            ray_copy(w).wait_send()
            beam_copy(w).wait_send()


def image_kernel(u, gauss, step, beams, image, v):
    total = jnp.zeros((XW, image.shape[0]), jnp.float32)
    for w in range(WIN):
        here = beams[w].astype(jnp.float32)
        g = gauss[w]
        for chunk in range(STEPS):
            if chunk:
                g = g * step[w]
            for at in (2 * chunk, 2 * chunk + 1):
                v[w, at] = (g * here[at : at + 1]).astype(jnp.bfloat16)
        total += jnp.dot(
            jnp.concatenate([v[w, at] for at in range(2 * STEPS)], axis=1),
            jnp.concatenate([u[w, part] for part in range(u.shape[1])], axis=1),
            preferred_element_type=jnp.float32,
        )
    image[...] = total.T


def shards(traces, centre_ids, midpoint_bins, ray_times, ray_amps, beam_lateral, footprint):
    slabs = lax.axis_size("slab")
    count = traces.shape[1]
    depth = ray_times.shape[4]
    columns = 2 * NF * P_SIZE
    operands = (
        traces,
        centre_ids.reshape(1, count),
        midpoint_bins,
        jnp.asarray(dft_halves()),
        jnp.asarray(slant_halves()),
        jnp.asarray(spread_table()),
        ray_times,
        ray_amps,
        beam_lateral.transpose(0, 2, 3, 1),
        footprint.transpose(1, 2, 0),
    )
    vmem = pl.BlockSpec(memory_space=pltpu.VMEM)
    tables = pl.pallas_call(
        functools.partial(kernel, slabs, 1.0 / math.sqrt(NT * count)),
        out_shape=[
            jax.ShapeDtypeStruct((WIN, depth // 128, columns, 128), jnp.bfloat16),
            jax.ShapeDtypeStruct((WIN, XW, LANES), jnp.float32),
            jax.ShapeDtypeStruct((WIN, XW, LANES), jnp.float32),
            jax.ShapeDtypeStruct((WIN, 2 * STEPS, LANES), jnp.bfloat16),
        ],
        in_specs=[pl.BlockSpec(memory_space=pltpu.HBM)] * 10,
        out_specs=[vmem] * 4,
        scratch_shapes=[
            pltpu.VMEM((count, NT), jnp.bfloat16),
            pltpu.VMEM((1, count), jnp.int32),
            pltpu.VMEM((1, count), jnp.int32),
            pltpu.VMEM((4 * NF, NT), jnp.bfloat16),
            pltpu.VMEM((2 * STEPS, 2 * BINS, LANES), jnp.bfloat16),
            pltpu.VMEM((2, 4 * KLO, LANES), jnp.bfloat16),
            pltpu.VMEM((WIN, P_SIZE, slabs), jnp.float32),
            pltpu.VMEM((WIN, 2, slabs), jnp.int32),
            pltpu.VMEM((WIN, 2, P_SIZE, depth), jnp.float32),
            pltpu.VMEM((WIN, 2, P_SIZE, depth), jnp.float32),
            pltpu.VMEM((slabs, 2 * STEPS, LANES), jnp.float32),
            pltpu.VMEM((slabs, 2 * STEPS, LANES), jnp.bfloat16),
            pltpu.VMEM((slabs, 2 * STEPS, LANES), jnp.bfloat16),
            pltpu.SemaphoreType.DMA((10,)),
            pltpu.SemaphoreType.DMA,
            pltpu.SemaphoreType.DMA,
            pltpu.SemaphoreType.DMA((WIN,)),
            pltpu.SemaphoreType.DMA((WIN,)),
            pltpu.SemaphoreType.DMA((WIN,)),
            pltpu.SemaphoreType.DMA((WIN,)),
        ],
        compiler_params=pltpu.CompilerParams(
            collective_id=0, has_side_effects=True, vmem_limit_bytes=24 * 1024 * 1024
        ),
    )(*[pltpu.with_memory_space_constraint(operand, pltpu.HBM) for operand in operands])
    partial_image = pl.pallas_call(
        image_kernel,
        out_shape=jax.ShapeDtypeStruct((depth, XW), jnp.float32),
        in_specs=[vmem] * 4,
        out_specs=vmem,
        scratch_shapes=[pltpu.VMEM((WIN, 2 * STEPS, XW, LANES), jnp.bfloat16)],
        compiler_params=pltpu.CompilerParams(vmem_limit_bytes=24 * 1024 * 1024),
    )(*tables)
    if lax.axis_size("offset") == 1:
        return partial_image
    return lax.psum_scatter(partial_image, "offset", scatter_dimension=0, tiled=True)


def solution(mesh):
    return jax.shard_map(
        shards,
        mesh=mesh,
        in_specs=(
            P("offset", "slab", None),
            P("offset", "slab", None),
            P("offset", "slab"),
            P("offset", "slab", None, None, None),
            P("offset", "slab", None, None, None),
            P("offset", None, None, None),
            P(),
        ),
        out_specs=P("offset", "slab"),
        check_vma=False,
    )
```

```python
import functools
import math

import jax
import jax.numpy as jnp
import ml_dtypes
import numpy as np
from jax import lax
from jax.experimental import pallas as pl
from jax.experimental.pallas import tpu as pltpu
from jax.sharding import PartitionSpec as P

NT = 256
NF = 64
KLO = 8
P_SIZE = 16
BINS = 16
WIN = 7
XW = 128
HALF = (WIN - 1) // 2
STEPS = NF // KLO
LANES = KLO * P_SIZE
GROUP = 8

slow_step = 0.25
width_scale = 200.0

def order(i):
    return HALF + (i + 1) // 2 * (1 - 2 * (i % 2))


OTHERS = [order(i) for i in range(1, WIN)]


def halves(table):
    high = table.astype(ml_dtypes.bfloat16)
    low = (table - high.astype(np.float64)).astype(ml_dtypes.bfloat16)
    return high, low


def dft_halves():
    turns = np.outer(np.arange(NT), np.arange(NF) + KLO) % NT * (2.0 * np.pi / NT)
    return np.concatenate(halves(np.concatenate([np.cos(turns), -np.sin(turns)], axis=1)), axis=1)


def by_chunk(table):
    rows = table.shape[0]
    return table.reshape(rows, 2, STEPS, LANES).transpose(2, 1, 0, 3).reshape(-1, rows, LANES)


def slant_halves():
    omega = (np.arange(NF) + KLO) * (2.0 * np.pi / NT)
    slow = (np.arange(P_SIZE) - (P_SIZE - 1) / 2.0) * slow_step
    place = np.arange(BINS) - (BINS - 1) / 2.0
    phase = place[:, None] * (omega[:, None] * slow[None, :]).reshape(1, -1)
    table = by_chunk(np.concatenate([np.cos(phase), np.sin(phase)], axis=1))
    return np.concatenate(halves(table), axis=1)


def spread_table():
    return by_chunk(np.repeat(np.eye(2 * NF), P_SIZE, axis=1)).astype(ml_dtypes.bfloat16)


def fit_even(values, degree):
    nodes = 0.125 - 0.125 * np.cos((np.arange(400) + 0.5) * np.pi / 400)
    poly = np.polynomial.chebyshev.Chebyshev.fit(nodes, values(np.sqrt(nodes)), degree, domain=[0, 0.25])
    return [float(c) for c in poly.convert(kind=np.polynomial.Polynomial).coef]


COS_FIT = fit_even(lambda y: np.cos(2 * np.pi * y), 7)
SIN_FIT = fit_even(lambda y: np.sin(2 * np.pi * y) / y, 6)


def horner(fit, s):
    total = jnp.full_like(s, fit[-1])
    for c in fit[-2::-1]:
        total = total * s + c
    return total


def turn(y):
    y = y - jnp.floor(y + 0.5)
    s = y * y
    return horner(COS_FIT, s), horner(SIN_FIT, s) * y


def pair(ref, at):
    return jnp.concatenate([ref[at], ref[at + 1]], axis=1)


def kernel(
    slabs, scale,
    traces_in, ids_in, bins_in, dft_in, slant_in, spread_in, times_in, amps_in, lateral_in, footprint_in,
    u, gauss, step, beams,
    traces, ids, bins, dft, slant, spread, lateral, footprint,
    rays, rays_here, sums, send, arrived, group_sum, group_send, group_arrived,
    load_sem, send_sem, recv_sem, peer_send, peer_recv, ray_send, ray_recv, beam_send, beam_recv,
):
    me = lax.axis_index("slab")
    parts = u.shape[1]

    def slab_at(k):
        return lax.rem(me + k, slabs)

    def goes(w):
        target = me + (w - HALF)
        return (target >= 0) & (target < slabs)

    def comes(w):
        source = me - (w - HALF)
        return (source >= 0) & (source < slabs)

    groups = slabs // GROUP
    group = me // GROUP
    base = group * GROUP
    spot = lax.rem(me, GROUP)

    def mate(k):
        return base + lax.rem(spot + k, GROUP)

    def peer(k):
        return lax.rem(group + k, groups) * GROUP + spot

    loads = [
        pltpu.make_async_copy(source, held, load_sem.at[i])
        for i, (source, held) in enumerate(
            (
                (traces_in.at[0], traces),
                (dft_in, dft),
                (ids_in, ids),
                (bins_in, bins),
                (slant_in, slant),
                (spread_in, spread),
                (times_in.at[0, 0], rays.at[:, 0]),
                (amps_in.at[0, 0], rays.at[:, 1]),
                (lateral_in.at[0], lateral),
                (footprint_in, footprint),
            )
        )
    ]
    for load in loads:
        load.start()

    barrier = pltpu.get_barrier_semaphore()

    def greet(target):
        pl.semaphore_signal(
            barrier, inc=1, device_id={"slab": target}, device_id_type=pl.DeviceIdType.MESH
        )

    for k in range(1, GROUP):
        greet(mate(k))
    for k in range(1, groups):
        greet(peer(k))
    greetings = GROUP - 1 + groups - 1
    for w in OTHERS:

        @pl.when(goes(w))
        def _():
            greet(slab_at(slabs + w - HALF))

        greetings = greetings + jnp.where(goes(w), 1, 0)

    def mate_copy(k):
        return pltpu.make_async_remote_copy(
            src_ref=send.at[pl.ds(lax.rem(spot + k, GROUP) * groups, groups)],
            dst_ref=arrived.at[k],
            send_sem=send_sem.at[k],
            recv_sem=recv_sem.at[k],
            device_id={"slab": mate(k)},
            device_id_type=pl.DeviceIdType.MESH,
        )

    def peer_copy(k):
        return pltpu.make_async_remote_copy(
            src_ref=group_send.at[lax.rem(group + k, groups)],
            dst_ref=group_arrived.at[k],
            send_sem=peer_send.at[k],
            recv_sem=peer_recv.at[k],
            device_id={"slab": peer(k)},
            device_id_type=pl.DeviceIdType.MESH,
        )

    def ray_copy(w):
        return pltpu.make_async_remote_copy(
            src_ref=rays.at[w],
            dst_ref=rays_here.at[w],
            send_sem=ray_send.at[w],
            recv_sem=ray_recv.at[w],
            device_id={"slab": slab_at(slabs + w - HALF)},
            device_id_type=pl.DeviceIdType.MESH,
        )

    def beam_copy(w):
        return pltpu.make_async_remote_copy(
            src_ref=beams.at[HALF],
            dst_ref=beams.at[w],
            send_sem=beam_send.at[w],
            recv_sem=beam_recv.at[w],
            device_id={"slab": slab_at(slabs + w - HALF)},
            device_id_type=pl.DeviceIdType.MESH,
        )

    def send_rays(slots):
        for w in slots:

            @pl.when(goes(w))
            def _():
                ray_copy(w).start()

    for load in loads[:4]:
        load.wait()
    spectrum = jnp.dot(traces[...], dft[...], preferred_element_type=jnp.float32)
    spec = (spectrum[:, : 2 * NF] + spectrum[:, 2 * NF :]).astype(jnp.bfloat16)
    count = spec.shape[0]
    bin_row = lax.broadcasted_iota(jnp.int32, (2 * BINS, count), 0) % BINS
    bin_hot = jnp.where(bin_row == bins[...], 1.0, 0.0).T.astype(jnp.bfloat16)
    id_row = lax.broadcasted_iota(jnp.int32, (slabs, count), 0)
    id_at = ids[...] % GROUP * groups + ids[...] // GROUP
    id_hot = jnp.where(id_row == id_at, 1.0, 0.0).astype(jnp.bfloat16)
    for load in loads[4:8]:
        load.wait()

    pl.semaphore_wait(barrier, greetings)
    send_rays(OTHERS)
    for w in OTHERS:

        @pl.when(jnp.logical_not(comes(w)))
        def _():
            rays_here[w] = rays[w]
            beams[w] = jnp.zeros_like(beams[w])

    for chunk in range(STEPS):
        spec_wide = jnp.dot(spec, pair(spread, 2 * chunk), preferred_element_type=jnp.float32)
        turn_wide = jnp.dot(bin_hot, pair(slant, 2 * chunk), preferred_element_type=jnp.float32)
        spec_re, spec_im = spec_wide[:, :LANES], spec_wide[:, LANES:]
        cosine, sine = turn_wide[:, :LANES], turn_wide[:, LANES:]
        terms = jnp.concatenate(
            [spec_re * cosine + spec_im * sine, spec_im * cosine - spec_re * sine], axis=1
        )
        partial = jnp.dot(id_hot, terms.astype(jnp.bfloat16), preferred_element_type=jnp.float32)
        sums[:, 2 * chunk, :] = partial[:, :LANES] * scale
        sums[:, 2 * chunk + 1, :] = partial[:, LANES:] * scale
    send[...] = sums[...].astype(jnp.bfloat16)
    for k in range(1, GROUP):
        mate_copy(k).start()

    def make_u(w, held):
        for part in range(parts):
            z = slice(part * 128, (part + 1) * 128)
            make_u_part(w, part, held[w, 0, :, z], held[w, 1, :, z])

    def make_u_part(w, part, t, a):
        cos8, sin8 = turn(t * (KLO / NT))
        cos1, sin1 = turn(t * (1.0 / NT))
        twice = 2.0 * cos8
        re, im = a, jnp.zeros_like(a)
        for b in range(KLO):
            if b:
                re, im = re * cos1 + im * sin1, im * cos1 - re * sin1
            last_re, last_im = re, im
            now_re, now_im = re * cos8 + im * sin8, im * cos8 - re * sin8
            for chunk in range(STEPS):
                at = 2 * chunk * LANES + b * P_SIZE
                u[w, part, at : at + P_SIZE, :] = now_re.astype(jnp.bfloat16)
                u[w, part, at + LANES : at + LANES + P_SIZE, :] = now_im.astype(jnp.bfloat16)
                if chunk < STEPS - 1:
                    now_re, last_re = twice * now_re - last_re, now_re
                    now_im, last_im = twice * now_im - last_im, now_im

    lane = lax.broadcasted_iota(jnp.int32, (1, LANES), 1)
    place = lax.broadcasted_iota(jnp.int32, (XW, LANES), 0).astype(jnp.float32)
    slow_row = lax.broadcasted_iota(jnp.int32, (P_SIZE, LANES), 0)
    slow_lane = lax.broadcasted_iota(jnp.int32, (P_SIZE, LANES), 1) % P_SIZE
    rate = -2.0 * math.pi / NT / width_scale * math.log2(math.e)
    rates = (lane // P_SIZE + KLO).astype(jnp.float32) * rate

    def pick(values, w):
        centre = jnp.clip(me - (w - HALF), 0, slabs - 1)
        held = lax.broadcasted_iota(jnp.int32, values.shape, 1) == centre
        return jnp.sum(jnp.where(held, values, 0.0), axis=1, keepdims=True)

    def make_gauss(w, carry):
        axis = pick(lateral[w], w)
        axis = jnp.sum(jnp.where(slow_row == slow_lane, axis, 0.0), axis=0, keepdims=True)
        ends = pick(footprint[w].astype(jnp.float32), w)
        off = place - axis
        off = jnp.where((place >= ends[0:1]) & (place < ends[1:2]), off * off, 1e9)
        gauss[w] = jnp.exp2(off * rates) * (1.0 / math.sqrt(P_SIZE * NF))
        step[w] = jnp.exp2(off * (KLO * rate))
        return carry

    def take_rays(i, carry):
        w = order(i)

        @pl.when(comes(w) & (w != HALF))
        def _():
            ray_copy(w).wait_recv()

        make_u(w, rays_here)
        return carry

    rays_here[HALF] = rays[HALF]
    for load in loads[8:]:
        load.wait()
    lax.fori_loop(0, WIN, make_gauss, 0)
    lax.fori_loop(0, 2, take_rays, 0)

    for k in range(1, GROUP):
        mate_copy(k).wait_recv()
    group_sum[...] = send[pl.ds(spot * groups, groups)].astype(jnp.float32) + jnp.sum(
        arrived[1:].astype(jnp.float32), axis=0
    )
    group_send[...] = group_sum[...].astype(jnp.bfloat16)
    for k in range(1, groups):
        peer_copy(k).start()
    lax.fori_loop(2, 4, take_rays, 0)

    own = group_sum[group]
    for k in range(1, groups):
        peer_copy(k).wait_recv()
        own = own + group_arrived[k].astype(jnp.float32)
    beams[HALF] = own.astype(jnp.bfloat16)
    for w in OTHERS:

        @pl.when(goes(w))
        def _():
            beam_copy(w).start()

    lax.fori_loop(4, WIN, take_rays, 0)
    for w in OTHERS:

        @pl.when(comes(w))
        def _():
            beam_copy(w).wait_recv()

    for k in range(1, GROUP):
        mate_copy(k).wait_send()
    for k in range(1, groups):
        peer_copy(k).wait_send()
    for w in OTHERS:

        @pl.when(goes(w))
        def _():
            ray_copy(w).wait_send()
            beam_copy(w).wait_send()


def image_kernel(u, gauss, step, beams, image, v):
    total = jnp.zeros((XW, image.shape[0]), jnp.float32)
    for w in range(WIN):
        here = beams[w].astype(jnp.float32)
        g = gauss[w]
        for chunk in range(STEPS):
            if chunk:
                g = g * step[w]
            for at in (2 * chunk, 2 * chunk + 1):
                v[w, at] = (g * here[at : at + 1]).astype(jnp.bfloat16)
        total += jnp.dot(
            jnp.concatenate([v[w, at] for at in range(2 * STEPS)], axis=1),
            jnp.concatenate([u[w, part] for part in range(u.shape[1])], axis=1),
            preferred_element_type=jnp.float32,
        )
    image[...] = total.T


def shards(traces, centre_ids, midpoint_bins, ray_times, ray_amps, beam_lateral, footprint):
    slabs = lax.axis_size("slab")
    groups = slabs // GROUP
    count = traces.shape[1]
    depth = ray_times.shape[4]
    columns = 2 * NF * P_SIZE
    operands = (
        traces,
        centre_ids.reshape(1, count),
        midpoint_bins,
        jnp.asarray(dft_halves()),
        jnp.asarray(slant_halves()),
        jnp.asarray(spread_table()),
        ray_times,
        ray_amps,
        beam_lateral.transpose(0, 2, 3, 1),
        footprint.transpose(1, 2, 0),
    )
    vmem = pl.BlockSpec(memory_space=pltpu.VMEM)
    tables = pl.pallas_call(
        functools.partial(kernel, slabs, 1.0 / math.sqrt(NT * count)),
        out_shape=[
            jax.ShapeDtypeStruct((WIN, depth // 128, columns, 128), jnp.bfloat16),
            jax.ShapeDtypeStruct((WIN, XW, LANES), jnp.float32),
            jax.ShapeDtypeStruct((WIN, XW, LANES), jnp.float32),
            jax.ShapeDtypeStruct((WIN, 2 * STEPS, LANES), jnp.bfloat16),
        ],
        in_specs=[pl.BlockSpec(memory_space=pltpu.HBM)] * 10,
        out_specs=[vmem] * 4,
        scratch_shapes=[
            pltpu.VMEM((count, NT), jnp.bfloat16),
            pltpu.VMEM((1, count), jnp.int32),
            pltpu.VMEM((1, count), jnp.int32),
            pltpu.VMEM((NT, 4 * NF), jnp.bfloat16),
            pltpu.VMEM((2 * STEPS, 2 * BINS, LANES), jnp.bfloat16),
            pltpu.VMEM((2 * STEPS, 2 * NF, LANES), jnp.bfloat16),
            pltpu.VMEM((WIN, P_SIZE, slabs), jnp.float32),
            pltpu.VMEM((WIN, 2, slabs), jnp.int32),
            pltpu.VMEM((WIN, 2, P_SIZE, depth), jnp.float32),
            pltpu.VMEM((WIN, 2, P_SIZE, depth), jnp.float32),
            pltpu.VMEM((slabs, 2 * STEPS, LANES), jnp.float32),
            pltpu.VMEM((slabs, 2 * STEPS, LANES), jnp.bfloat16),
            pltpu.VMEM((GROUP, groups, 2 * STEPS, LANES), jnp.bfloat16),
            pltpu.VMEM((groups, 2 * STEPS, LANES), jnp.float32),
            pltpu.VMEM((groups, 2 * STEPS, LANES), jnp.bfloat16),
            pltpu.VMEM((groups, 2 * STEPS, LANES), jnp.bfloat16),
            pltpu.SemaphoreType.DMA((10,)),
            pltpu.SemaphoreType.DMA((GROUP,)),
            pltpu.SemaphoreType.DMA((GROUP,)),
            pltpu.SemaphoreType.DMA((groups,)),
            pltpu.SemaphoreType.DMA((groups,)),
            pltpu.SemaphoreType.DMA((WIN,)),
            pltpu.SemaphoreType.DMA((WIN,)),
            pltpu.SemaphoreType.DMA((WIN,)),
            pltpu.SemaphoreType.DMA((WIN,)),
        ],
        compiler_params=pltpu.CompilerParams(
            collective_id=0, has_side_effects=True, vmem_limit_bytes=24 * 1024 * 1024
        ),
    )(*[pltpu.with_memory_space_constraint(operand, pltpu.HBM) for operand in operands])
    partial_image = pl.pallas_call(
        image_kernel,
        out_shape=jax.ShapeDtypeStruct((depth, XW), jnp.float32),
        in_specs=[vmem] * 4,
        out_specs=vmem,
        scratch_shapes=[pltpu.VMEM((WIN, 2 * STEPS, XW, LANES), jnp.bfloat16)],
        compiler_params=pltpu.CompilerParams(vmem_limit_bytes=24 * 1024 * 1024),
    )(*tables)
    if lax.axis_size("offset") == 1:
        return partial_image
    return lax.psum_scatter(partial_image, "offset", scatter_dimension=0, tiled=True)


def solution(mesh):
    return jax.shard_map(
        shards,
        mesh=mesh,
        in_specs=(
            P("offset", "slab", None),
            P("offset", "slab", None),
            P("offset", "slab"),
            P("offset", "slab", None, None, None),
            P("offset", "slab", None, None, None),
            P("offset", None, None, None),
            P(),
        ),
        out_specs=P("offset", "slab"),
        check_vma=False,
    )
```

```python
import functools
import math

import jax
import jax.numpy as jnp
import ml_dtypes
import numpy as np
from jax import lax
from jax.experimental import pallas as pl
from jax.experimental.pallas import tpu as pltpu
from jax.sharding import PartitionSpec as P

NT = 256
NF = 64
KLO = 8
P_SIZE = 16
BINS = 16
WIN = 7
XW = 128
HALF = (WIN - 1) // 2
STEPS = NF // KLO
LANES = KLO * P_SIZE

slow_step = 0.25
width_scale = 200.0

def order(i):
    return HALF + (i + 1) // 2 * (1 - 2 * (i % 2))


OTHERS = [order(i) for i in range(1, WIN)]


def halves(table):
    high = table.astype(ml_dtypes.bfloat16)
    low = (table - high.astype(np.float64)).astype(ml_dtypes.bfloat16)
    return high, low


def dft_halves():
    turns = np.outer(np.arange(NT), np.arange(NF) + KLO) % NT * (2.0 * np.pi / NT)
    return np.concatenate(halves(np.concatenate([np.cos(turns), -np.sin(turns)], axis=1)), axis=1)


def by_chunk(table):
    rows = table.shape[0]
    return table.reshape(rows, 2, STEPS, LANES).transpose(2, 1, 0, 3).reshape(-1, rows, LANES)


def slant_halves():
    omega = (np.arange(NF) + KLO) * (2.0 * np.pi / NT)
    slow = (np.arange(P_SIZE) - (P_SIZE - 1) / 2.0) * slow_step
    place = np.arange(BINS) - (BINS - 1) / 2.0
    phase = place[:, None] * (omega[:, None] * slow[None, :]).reshape(1, -1)
    table = by_chunk(np.concatenate([np.cos(phase), np.sin(phase)], axis=1))
    return np.concatenate(halves(table), axis=1)


def spread_table():
    one_of = by_chunk(np.repeat(np.eye(2 * NF), P_SIZE, axis=1))
    return np.concatenate([one_of, one_of], axis=1).astype(ml_dtypes.bfloat16)


def fit_even(values, degree):
    nodes = 0.125 - 0.125 * np.cos((np.arange(400) + 0.5) * np.pi / 400)
    poly = np.polynomial.chebyshev.Chebyshev.fit(nodes, values(np.sqrt(nodes)), degree, domain=[0, 0.25])
    return [float(c) for c in poly.convert(kind=np.polynomial.Polynomial).coef]


COS_FIT = fit_even(lambda y: np.cos(2 * np.pi * y), 7)
SIN_FIT = fit_even(lambda y: np.sin(2 * np.pi * y) / y, 6)


def horner(fit, s):
    total = jnp.full_like(s, fit[-1])
    for c in fit[-2::-1]:
        total = total * s + c
    return total


def turn(y):
    y = y - jnp.floor(y + 0.5)
    s = y * y
    return horner(COS_FIT, s), horner(SIN_FIT, s) * y


def pair(ref, at):
    return jnp.concatenate([ref[at], ref[at + 1]], axis=1)


def kernel(
    slabs, scale,
    traces_in, ids_in, bins_in, dft_in, slant_in, spread_in, times_in, amps_in, lateral_in, footprint_in,
    u, gauss, step, beams,
    traces, ids, bins, dft, slant, spread, lateral, footprint,
    rays, rays_here, sums, send, arrived,
    load_sem, send_sem, recv_sem, ray_send, ray_recv, beam_send, beam_recv,
):
    me = lax.axis_index("slab")
    parts = u.shape[1]

    def slab_at(k):
        return lax.rem(me + k, slabs)

    loads = [
        pltpu.make_async_copy(source, held, load_sem.at[i])
        for i, (source, held) in enumerate(
            (
                (traces_in.at[0], traces),
                (dft_in, dft),
                (ids_in, ids),
                (bins_in, bins),
                (slant_in, slant),
                (spread_in, spread),
                (times_in.at[0, 0], rays.at[:, 0]),
                (amps_in.at[0, 0], rays.at[:, 1]),
                (lateral_in.at[0], lateral),
                (footprint_in, footprint),
            )
        )
    ]
    for load in loads:
        load.start()

    barrier = pltpu.get_barrier_semaphore()

    def greet(k, carry):
        pl.semaphore_signal(barrier, inc=1, device_id={"slab": slab_at(k)}, device_id_type=pl.DeviceIdType.MESH)
        return carry

    lax.fori_loop(1, slabs, greet, 0)

    def block_copies(first, count):
        return pltpu.make_async_remote_copy(
            src_ref=send.at[pl.ds(slab_at(first), count)] if count == 1 else send.at[pl.ds(0, count)],
            dst_ref=arrived.at[pl.ds(first, count)],
            send_sem=send_sem,
            recv_sem=recv_sem,
            device_id={"slab": slab_at(first)},
            device_id_type=pl.DeviceIdType.MESH,
        )

    def start_block(k, carry):
        block_copies(k, 1).start()
        return carry

    def ray_copy(w):
        return pltpu.make_async_remote_copy(
            src_ref=rays.at[w],
            dst_ref=rays_here.at[w],
            send_sem=ray_send.at[w],
            recv_sem=ray_recv.at[w],
            device_id={"slab": slab_at(slabs + w - HALF)},
            device_id_type=pl.DeviceIdType.MESH,
        )

    def beam_copy(w):
        return pltpu.make_async_remote_copy(
            src_ref=beams.at[HALF],
            dst_ref=beams.at[w],
            send_sem=beam_send.at[w],
            recv_sem=beam_recv.at[w],
            device_id={"slab": slab_at(slabs + w - HALF)},
            device_id_type=pl.DeviceIdType.MESH,
        )

    def goes(w):
        target = me + (w - HALF)
        return (target >= 0) & (target < slabs)

    def comes(w):
        source = me - (w - HALF)
        return (source >= 0) & (source < slabs)

    def send_rays(slots):
        for w in slots:

            @pl.when(goes(w))
            def _():
                ray_copy(w).start()

    for load in loads[:4]:
        load.wait()
    spectrum = jnp.dot(traces[...], dft[...], preferred_element_type=jnp.float32)
    spectrum = spectrum[:, : 2 * NF] + spectrum[:, 2 * NF :]
    spec_high = spectrum.astype(jnp.bfloat16)
    spec_low = (spectrum - spec_high.astype(jnp.float32)).astype(jnp.bfloat16)
    spec = jnp.concatenate([spec_high, spec_low], axis=1)
    count = spec.shape[0]
    bin_row = lax.broadcasted_iota(jnp.int32, (2 * BINS, count), 0) % BINS
    bin_hot = jnp.where(bin_row == bins[...], 1.0, 0.0).T.astype(jnp.bfloat16)
    id_row = lax.broadcasted_iota(jnp.int32, (slabs, count), 0)
    id_hot = jnp.where(id_row == ids[...], 1.0, 0.0).astype(jnp.bfloat16)
    id_hot = jnp.concatenate([id_hot, id_hot], axis=1)
    for load in loads[4:8]:
        load.wait()

    pl.semaphore_wait(barrier, slabs - 1)
    send_rays(OTHERS[:2])
    for w in OTHERS:

        @pl.when(jnp.logical_not(comes(w)))
        def _():
            rays_here[w] = rays[w]
            beams[w] = jnp.zeros_like(beams[w])

    for chunk in range(STEPS):
        spec_wide = jnp.dot(spec, pair(spread, 2 * chunk), preferred_element_type=jnp.float32)
        turn_wide = jnp.dot(bin_hot, pair(slant, 2 * chunk), preferred_element_type=jnp.float32)
        spec_re, spec_im = spec_wide[:, :LANES], spec_wide[:, LANES:]
        cosine, sine = turn_wide[:, :LANES], turn_wide[:, LANES:]
        terms = jnp.concatenate(
            [spec_re * cosine + spec_im * sine, spec_im * cosine - spec_re * sine], axis=1
        )
        high = terms.astype(jnp.bfloat16)
        low = (terms - high.astype(jnp.float32)).astype(jnp.bfloat16)
        partial = jnp.dot(
            id_hot, jnp.concatenate([high, low], axis=0), preferred_element_type=jnp.float32
        )
        sums[:, 2 * chunk, :] = partial[:, :LANES] * scale
        sums[:, 2 * chunk + 1, :] = partial[:, LANES:] * scale
    send[...] = sums[...].astype(jnp.bfloat16)
    lax.fori_loop(1, slabs, start_block, 0)
    send_rays(OTHERS[2:])

    def make_u(w, held):
        for part in range(parts):
            z = slice(part * 128, (part + 1) * 128)
            make_u_part(w, part, held[w, 0, :, z], held[w, 1, :, z])

    def make_u_part(w, part, t, a):
        cos8, sin8 = turn(t * (KLO / NT))
        cos1, sin1 = turn(t * (1.0 / NT))
        twice = 2.0 * cos8
        re, im = a, jnp.zeros_like(a)
        for b in range(KLO):
            if b:
                re, im = re * cos1 + im * sin1, im * cos1 - re * sin1
            last_re, last_im = re, im
            now_re, now_im = re * cos8 + im * sin8, im * cos8 - re * sin8
            for chunk in range(STEPS):
                at = 2 * chunk * LANES + b * P_SIZE
                u[w, part, at : at + P_SIZE, :] = now_re.astype(jnp.bfloat16)
                u[w, part, at + LANES : at + LANES + P_SIZE, :] = now_im.astype(jnp.bfloat16)
                if chunk < STEPS - 1:
                    now_re, last_re = twice * now_re - last_re, now_re
                    now_im, last_im = twice * now_im - last_im, now_im

    lane = lax.broadcasted_iota(jnp.int32, (1, LANES), 1)
    place = lax.broadcasted_iota(jnp.int32, (XW, LANES), 0).astype(jnp.float32)
    slow_row = lax.broadcasted_iota(jnp.int32, (P_SIZE, LANES), 0)
    slow_lane = lax.broadcasted_iota(jnp.int32, (P_SIZE, LANES), 1) % P_SIZE
    rate = -2.0 * math.pi / NT / width_scale * math.log2(math.e)
    rates = (lane // P_SIZE + KLO).astype(jnp.float32) * rate

    def pick(values, w):
        centre = jnp.clip(me - (w - HALF), 0, slabs - 1)
        held = lax.broadcasted_iota(jnp.int32, values.shape, 1) == centre
        return jnp.sum(jnp.where(held, values, 0.0), axis=1, keepdims=True)

    def make_gauss(w, carry):
        axis = pick(lateral[w], w)
        axis = jnp.sum(jnp.where(slow_row == slow_lane, axis, 0.0), axis=0, keepdims=True)
        ends = pick(footprint[w].astype(jnp.float32), w)
        off = place - axis
        off = jnp.where((place >= ends[0:1]) & (place < ends[1:2]), off * off, 1e9)
        gauss[w] = jnp.exp2(off * rates) * (1.0 / math.sqrt(P_SIZE * NF))
        step[w] = jnp.exp2(off * (KLO * rate))
        return carry

    def take_rays(i, carry):
        w = order(i)

        @pl.when(comes(w) & (w != HALF))
        def _():
            ray_copy(w).wait_recv()

        make_u(w, rays_here)
        return carry

    rays_here[HALF] = rays[HALF]
    for load in loads[8:]:
        load.wait()
    lax.fori_loop(0, WIN, make_gauss, 0)
    lax.fori_loop(0, 3, take_rays, 0)

    arrived[0] = send[me]
    block_copies(1, slabs - 1).wait_recv()
    own = jnp.sum(arrived[...].astype(jnp.float32), axis=0)
    beams[HALF] = own.astype(jnp.bfloat16)
    for w in OTHERS:

        @pl.when(goes(w))
        def _():
            beam_copy(w).start()

    lax.fori_loop(3, WIN, take_rays, 0)
    for w in OTHERS:

        @pl.when(comes(w))
        def _():
            beam_copy(w).wait_recv()

    block_copies(1, slabs - 1).wait_send()
    for w in OTHERS:

        @pl.when(goes(w))
        def _():
            ray_copy(w).wait_send()
            beam_copy(w).wait_send()


def image_kernel(u, gauss, step, beams, image, v):
    total = jnp.zeros((XW, image.shape[0]), jnp.float32)
    for w in range(WIN):
        here = beams[w].astype(jnp.float32)
        g = gauss[w]
        for chunk in range(STEPS):
            if chunk:
                g = g * step[w]
            for at in (2 * chunk, 2 * chunk + 1):
                v[w, at] = (g * here[at : at + 1]).astype(jnp.bfloat16)
        total += jnp.dot(
            jnp.concatenate([v[w, at] for at in range(2 * STEPS)], axis=1),
            jnp.concatenate([u[w, part] for part in range(u.shape[1])], axis=1),
            preferred_element_type=jnp.float32,
        )
    image[...] = total.T


def shards(traces, centre_ids, midpoint_bins, ray_times, ray_amps, beam_lateral, footprint):
    slabs = lax.axis_size("slab")
    count = traces.shape[1]
    depth = ray_times.shape[4]
    columns = 2 * NF * P_SIZE
    operands = (
        traces,
        centre_ids.reshape(1, count),
        midpoint_bins,
        jnp.asarray(dft_halves()),
        jnp.asarray(slant_halves()),
        jnp.asarray(spread_table()),
        ray_times,
        ray_amps,
        beam_lateral.transpose(0, 2, 3, 1),
        footprint.transpose(1, 2, 0),
    )
    vmem = pl.BlockSpec(memory_space=pltpu.VMEM)
    tables = pl.pallas_call(
        functools.partial(kernel, slabs, 1.0 / math.sqrt(NT * count)),
        out_shape=[
            jax.ShapeDtypeStruct((WIN, depth // 128, columns, 128), jnp.bfloat16),
            jax.ShapeDtypeStruct((WIN, XW, LANES), jnp.float32),
            jax.ShapeDtypeStruct((WIN, XW, LANES), jnp.float32),
            jax.ShapeDtypeStruct((WIN, 2 * STEPS, LANES), jnp.bfloat16),
        ],
        in_specs=[pl.BlockSpec(memory_space=pltpu.HBM)] * 10,
        out_specs=[vmem] * 4,
        scratch_shapes=[
            pltpu.VMEM((count, NT), jnp.bfloat16),
            pltpu.VMEM((1, count), jnp.int32),
            pltpu.VMEM((1, count), jnp.int32),
            pltpu.VMEM((NT, 4 * NF), jnp.bfloat16),
            pltpu.VMEM((2 * STEPS, 2 * BINS, LANES), jnp.bfloat16),
            pltpu.VMEM((2 * STEPS, 4 * NF, LANES), jnp.bfloat16),
            pltpu.VMEM((WIN, P_SIZE, slabs), jnp.float32),
            pltpu.VMEM((WIN, 2, slabs), jnp.int32),
            pltpu.VMEM((WIN, 2, P_SIZE, depth), jnp.float32),
            pltpu.VMEM((WIN, 2, P_SIZE, depth), jnp.float32),
            pltpu.VMEM((slabs, 2 * STEPS, LANES), jnp.float32),
            pltpu.VMEM((slabs, 2 * STEPS, LANES), jnp.bfloat16),
            pltpu.VMEM((slabs, 2 * STEPS, LANES), jnp.bfloat16),
            pltpu.SemaphoreType.DMA((10,)),
            pltpu.SemaphoreType.DMA,
            pltpu.SemaphoreType.DMA,
            pltpu.SemaphoreType.DMA((WIN,)),
            pltpu.SemaphoreType.DMA((WIN,)),
            pltpu.SemaphoreType.DMA((WIN,)),
            pltpu.SemaphoreType.DMA((WIN,)),
        ],
        compiler_params=pltpu.CompilerParams(
            collective_id=0, has_side_effects=True, vmem_limit_bytes=24 * 1024 * 1024
        ),
    )(*[pltpu.with_memory_space_constraint(operand, pltpu.HBM) for operand in operands])
    partial_image = pl.pallas_call(
        image_kernel,
        out_shape=jax.ShapeDtypeStruct((depth, XW), jnp.float32),
        in_specs=[vmem] * 4,
        out_specs=vmem,
        scratch_shapes=[pltpu.VMEM((WIN, 2 * STEPS, XW, LANES), jnp.bfloat16)],
        compiler_params=pltpu.CompilerParams(vmem_limit_bytes=24 * 1024 * 1024),
    )(*tables)
    if lax.axis_size("offset") == 1:
        return partial_image
    return lax.psum_scatter(partial_image, "offset", scatter_dimension=0, tiled=True)


def solution(mesh):
    return jax.shard_map(
        shards,
        mesh=mesh,
        in_specs=(
            P("offset", "slab", None),
            P("offset", "slab", None),
            P("offset", "slab"),
            P("offset", "slab", None, None, None),
            P("offset", "slab", None, None, None),
            P("offset", None, None, None),
            P(),
        ),
        out_specs=P("offset", "slab"),
        check_vma=False,
    )
```

```python
import functools
import math

import jax
import jax.numpy as jnp
import ml_dtypes
import numpy as np
from jax import lax
from jax.experimental import pallas as pl
from jax.experimental.pallas import tpu as pltpu
from jax.sharding import PartitionSpec as P

NT = 256
NF = 64
KLO = 8
P_SIZE = 16
BINS = 16
WIN = 7
XW = 128
HALF = (WIN - 1) // 2
STEPS = NF // KLO
LANES = KLO * P_SIZE

slow_step = 0.25
width_scale = 200.0

def order(i):
    return HALF + (i + 1) // 2 * (1 - 2 * (i % 2))


OTHERS = [order(i) for i in range(1, WIN)]


def halves(table):
    high = table.astype(ml_dtypes.bfloat16)
    low = (table - high.astype(np.float64)).astype(ml_dtypes.bfloat16)
    return high, low


def dft_halves():
    turns = np.outer(np.arange(NT), np.arange(NF) + KLO) % NT * (2.0 * np.pi / NT)
    return np.concatenate(halves(np.concatenate([np.cos(turns), -np.sin(turns)], axis=1)), axis=1)


def by_chunk(table):
    rows = table.shape[0]
    return table.reshape(rows, 2, STEPS, LANES).transpose(2, 1, 0, 3).reshape(-1, rows, LANES)


def slant_halves():
    omega = (np.arange(NF) + KLO) * (2.0 * np.pi / NT)
    slow = (np.arange(P_SIZE) - (P_SIZE - 1) / 2.0) * slow_step
    place = np.arange(BINS) - (BINS - 1) / 2.0
    phase = place[:, None] * (omega[:, None] * slow[None, :]).reshape(1, -1)
    table = by_chunk(np.concatenate([np.cos(phase), np.sin(phase)], axis=1))
    return np.concatenate(halves(table), axis=1)


def spread_table():
    return by_chunk(np.repeat(np.eye(2 * NF), P_SIZE, axis=1)).astype(ml_dtypes.bfloat16)


def fit_even(values, degree):
    nodes = 0.125 - 0.125 * np.cos((np.arange(400) + 0.5) * np.pi / 400)
    poly = np.polynomial.chebyshev.Chebyshev.fit(nodes, values(np.sqrt(nodes)), degree, domain=[0, 0.25])
    return [float(c) for c in poly.convert(kind=np.polynomial.Polynomial).coef]


COS_FIT = fit_even(lambda y: np.cos(2 * np.pi * y), 7)
SIN_FIT = fit_even(lambda y: np.sin(2 * np.pi * y) / y, 6)


def horner(fit, s):
    total = jnp.full_like(s, fit[-1])
    for c in fit[-2::-1]:
        total = total * s + c
    return total


def turn(y):
    y = y - jnp.floor(y + 0.5)
    s = y * y
    return horner(COS_FIT, s), horner(SIN_FIT, s) * y


def pair(ref, at):
    return jnp.concatenate([ref[at], ref[at + 1]], axis=1)


def kernel(
    slabs, scale,
    traces_in, ids_in, bins_in, dft_in, slant_in, spread_in, times_in, amps_in, lateral_in, footprint_in,
    u, gauss, step, beams,
    traces, ids, bins, dft, slant, spread, lateral, footprint,
    rays, rays_here, sums, send, arrived,
    load_sem, send_sem, recv_sem, ray_send, ray_recv, beam_send, beam_recv,
):
    me = lax.axis_index("slab")
    parts = u.shape[1]

    def slab_at(k):
        return lax.rem(me + k, slabs)

    loads = [
        pltpu.make_async_copy(source, held, load_sem.at[i])
        for i, (source, held) in enumerate(
            (
                (traces_in.at[0], traces),
                (dft_in, dft),
                (ids_in, ids),
                (bins_in, bins),
                (slant_in, slant),
                (spread_in, spread),
                (times_in.at[0, 0], rays.at[:, 0]),
                (amps_in.at[0, 0], rays.at[:, 1]),
                (lateral_in.at[0], lateral),
                (footprint_in, footprint),
            )
        )
    ]
    for load in loads:
        load.start()

    barrier = pltpu.get_barrier_semaphore()

    def greet(k, carry):
        pl.semaphore_signal(barrier, inc=1, device_id={"slab": slab_at(k)}, device_id_type=pl.DeviceIdType.MESH)
        return carry

    lax.fori_loop(1, slabs, greet, 0)

    def block_copies(first, count):
        return pltpu.make_async_remote_copy(
            src_ref=send.at[pl.ds(slab_at(first), count)] if count == 1 else send.at[pl.ds(0, count)],
            dst_ref=arrived.at[pl.ds(first, count)],
            send_sem=send_sem,
            recv_sem=recv_sem,
            device_id={"slab": slab_at(first)},
            device_id_type=pl.DeviceIdType.MESH,
        )

    def start_block(k, carry):
        block_copies(k, 1).start()
        return carry

    def ray_copy(w):
        return pltpu.make_async_remote_copy(
            src_ref=rays.at[w],
            dst_ref=rays_here.at[w],
            send_sem=ray_send.at[w],
            recv_sem=ray_recv.at[w],
            device_id={"slab": slab_at(slabs + w - HALF)},
            device_id_type=pl.DeviceIdType.MESH,
        )

    def beam_copy(w):
        return pltpu.make_async_remote_copy(
            src_ref=beams.at[HALF],
            dst_ref=beams.at[w],
            send_sem=beam_send.at[w],
            recv_sem=beam_recv.at[w],
            device_id={"slab": slab_at(slabs + w - HALF)},
            device_id_type=pl.DeviceIdType.MESH,
        )

    def goes(w):
        target = me + (w - HALF)
        return (target >= 0) & (target < slabs)

    def comes(w):
        source = me - (w - HALF)
        return (source >= 0) & (source < slabs)

    def send_rays(slots):
        for w in slots:

            @pl.when(goes(w))
            def _():
                ray_copy(w).start()

    for load in loads[:4]:
        load.wait()
    spectrum = jnp.dot(traces[...], dft[...], preferred_element_type=jnp.float32)
    spectrum = spectrum[:, : 2 * NF] + spectrum[:, 2 * NF :]
    spec_high = spectrum.astype(jnp.bfloat16)
    spec_low = (spectrum - spec_high.astype(jnp.float32)).astype(jnp.bfloat16)
    spec = jnp.concatenate([spec_high, spec_low], axis=1)
    count = spec.shape[0]
    bin_row = lax.broadcasted_iota(jnp.int32, (2 * BINS, count), 0) % BINS
    bin_hot = jnp.where(bin_row == bins[...], 1.0, 0.0).T.astype(jnp.bfloat16)
    id_row = lax.broadcasted_iota(jnp.int32, (slabs, count), 0)
    id_hot = jnp.where(id_row == ids[...], 1.0, 0.0).astype(jnp.bfloat16)
    id_hot = jnp.concatenate([id_hot, id_hot], axis=1)
    for load in loads[4:8]:
        load.wait()

    pl.semaphore_wait(barrier, slabs - 1)
    send_rays(OTHERS[:2])
    for w in OTHERS:

        @pl.when(jnp.logical_not(comes(w)))
        def _():
            rays_here[w] = rays[w]
            beams[w] = jnp.zeros_like(beams[w])

    for chunk in range(STEPS):
        spread_wide = pair(spread, 2 * chunk)
        spec_wide = jnp.dot(
            spec,
            jnp.concatenate([spread_wide, spread_wide], axis=0),
            preferred_element_type=jnp.float32,
        )
        turn_wide = jnp.dot(bin_hot, pair(slant, 2 * chunk), preferred_element_type=jnp.float32)
        spec_re, spec_im = spec_wide[:, :LANES], spec_wide[:, LANES:]
        cosine, sine = turn_wide[:, :LANES], turn_wide[:, LANES:]
        terms = jnp.concatenate(
            [spec_re * cosine + spec_im * sine, spec_im * cosine - spec_re * sine], axis=1
        )
        high = terms.astype(jnp.bfloat16)
        low = (terms - high.astype(jnp.float32)).astype(jnp.bfloat16)
        partial = jnp.dot(
            id_hot, jnp.concatenate([high, low], axis=0), preferred_element_type=jnp.float32
        )
        sums[:, 2 * chunk, :] = partial[:, :LANES] * scale
        sums[:, 2 * chunk + 1, :] = partial[:, LANES:] * scale
    send[...] = sums[...].astype(jnp.bfloat16)
    lax.fori_loop(1, slabs, start_block, 0)
    send_rays(OTHERS[2:])

    def make_u(w, held):
        for part in range(parts):
            z = slice(part * 128, (part + 1) * 128)
            make_u_part(w, part, held[w, 0, :, z], held[w, 1, :, z])

    def make_u_part(w, part, t, a):
        cos8, sin8 = turn(t * (KLO / NT))
        cos1, sin1 = turn(t * (1.0 / NT))
        twice = 2.0 * cos8
        re, im = a, jnp.zeros_like(a)
        for b in range(KLO):
            if b:
                re, im = re * cos1 + im * sin1, im * cos1 - re * sin1
            last_re, last_im = re, im
            now_re, now_im = re * cos8 + im * sin8, im * cos8 - re * sin8
            for chunk in range(STEPS):
                at = 2 * chunk * LANES + b * P_SIZE
                u[w, part, at : at + P_SIZE, :] = now_re.astype(jnp.bfloat16)
                u[w, part, at + LANES : at + LANES + P_SIZE, :] = now_im.astype(jnp.bfloat16)
                if chunk < STEPS - 1:
                    now_re, last_re = twice * now_re - last_re, now_re
                    now_im, last_im = twice * now_im - last_im, now_im

    lane = lax.broadcasted_iota(jnp.int32, (1, LANES), 1)
    place = lax.broadcasted_iota(jnp.int32, (XW, LANES), 0).astype(jnp.float32)
    slow_row = lax.broadcasted_iota(jnp.int32, (P_SIZE, LANES), 0)
    slow_lane = lax.broadcasted_iota(jnp.int32, (P_SIZE, LANES), 1) % P_SIZE
    rate = -2.0 * math.pi / NT / width_scale * math.log2(math.e)
    rates = (lane // P_SIZE + KLO).astype(jnp.float32) * rate

    def pick(values, w):
        centre = jnp.clip(me - (w - HALF), 0, slabs - 1)
        held = lax.broadcasted_iota(jnp.int32, values.shape, 1) == centre
        return jnp.sum(jnp.where(held, values, 0.0), axis=1, keepdims=True)

    def make_gauss(w):
        axis = pick(lateral[w], w)
        axis = jnp.sum(jnp.where(slow_row == slow_lane, axis, 0.0), axis=0, keepdims=True)
        ends = pick(footprint[w].astype(jnp.float32), w)
        off = place - axis
        off = jnp.where((place >= ends[0:1]) & (place < ends[1:2]), off * off, 1e9)
        gauss[w] = jnp.exp2(off * rates) * (1.0 / math.sqrt(P_SIZE * NF))
        step[w] = jnp.exp2(off * (KLO * rate))

    def take_rays(i, carry):
        w = order(i)

        @pl.when(comes(w) & (w != HALF))
        def _():
            ray_copy(w).wait_recv()

        make_u(w, rays_here)
        return carry

    rays_here[HALF] = rays[HALF]
    for load in loads[8:]:
        load.wait()
    for w in range(WIN):
        make_gauss(w)
    lax.fori_loop(0, 3, take_rays, 0)

    arrived[0] = send[me]
    block_copies(1, slabs - 1).wait_recv()
    own = jnp.sum(arrived[...].astype(jnp.float32), axis=0)
    beams[HALF] = own.astype(jnp.bfloat16)
    for w in OTHERS:

        @pl.when(goes(w))
        def _():
            beam_copy(w).start()

    lax.fori_loop(3, WIN, take_rays, 0)
    for w in OTHERS:

        @pl.when(comes(w))
        def _():
            beam_copy(w).wait_recv()

    block_copies(1, slabs - 1).wait_send()
    for w in OTHERS:

        @pl.when(goes(w))
        def _():
            ray_copy(w).wait_send()
            beam_copy(w).wait_send()


def image_kernel(u, gauss, step, beams, image, v):
    total = jnp.zeros((XW, image.shape[0]), jnp.float32)
    for w in range(WIN):
        here = beams[w].astype(jnp.float32)
        g = gauss[w]
        for chunk in range(STEPS):
            if chunk:
                g = g * step[w]
            for at in (2 * chunk, 2 * chunk + 1):
                v[w, at] = (g * here[at : at + 1]).astype(jnp.bfloat16)
        total += jnp.dot(
            jnp.concatenate([v[w, at] for at in range(2 * STEPS)], axis=1),
            jnp.concatenate([u[w, part] for part in range(u.shape[1])], axis=1),
            preferred_element_type=jnp.float32,
        )
    image[...] = total.T


def shards(traces, centre_ids, midpoint_bins, ray_times, ray_amps, beam_lateral, footprint):
    slabs = lax.axis_size("slab")
    count = traces.shape[1]
    depth = ray_times.shape[4]
    columns = 2 * NF * P_SIZE
    operands = (
        traces,
        centre_ids.reshape(1, count),
        midpoint_bins,
        jnp.asarray(dft_halves()),
        jnp.asarray(slant_halves()),
        jnp.asarray(spread_table()),
        ray_times,
        ray_amps,
        beam_lateral.transpose(0, 2, 3, 1),
        footprint.transpose(1, 2, 0),
    )
    vmem = pl.BlockSpec(memory_space=pltpu.VMEM)
    tables = pl.pallas_call(
        functools.partial(kernel, slabs, 1.0 / math.sqrt(NT * count)),
        out_shape=[
            jax.ShapeDtypeStruct((WIN, depth // 128, columns, 128), jnp.bfloat16),
            jax.ShapeDtypeStruct((WIN, XW, LANES), jnp.float32),
            jax.ShapeDtypeStruct((WIN, XW, LANES), jnp.float32),
            jax.ShapeDtypeStruct((WIN, 2 * STEPS, LANES), jnp.bfloat16),
        ],
        in_specs=[pl.BlockSpec(memory_space=pltpu.HBM)] * 10,
        out_specs=[vmem] * 4,
        scratch_shapes=[
            pltpu.VMEM((count, NT), jnp.bfloat16),
            pltpu.VMEM((1, count), jnp.int32),
            pltpu.VMEM((1, count), jnp.int32),
            pltpu.VMEM((NT, 4 * NF), jnp.bfloat16),
            pltpu.VMEM((2 * STEPS, 2 * BINS, LANES), jnp.bfloat16),
            pltpu.VMEM((2 * STEPS, 2 * NF, LANES), jnp.bfloat16),
            pltpu.VMEM((WIN, P_SIZE, slabs), jnp.float32),
            pltpu.VMEM((WIN, 2, slabs), jnp.int32),
            pltpu.VMEM((WIN, 2, P_SIZE, depth), jnp.float32),
            pltpu.VMEM((WIN, 2, P_SIZE, depth), jnp.float32),
            pltpu.VMEM((slabs, 2 * STEPS, LANES), jnp.float32),
            pltpu.VMEM((slabs, 2 * STEPS, LANES), jnp.bfloat16),
            pltpu.VMEM((slabs, 2 * STEPS, LANES), jnp.bfloat16),
            pltpu.SemaphoreType.DMA((10,)),
            pltpu.SemaphoreType.DMA,
            pltpu.SemaphoreType.DMA,
            pltpu.SemaphoreType.DMA((WIN,)),
            pltpu.SemaphoreType.DMA((WIN,)),
            pltpu.SemaphoreType.DMA((WIN,)),
            pltpu.SemaphoreType.DMA((WIN,)),
        ],
        compiler_params=pltpu.CompilerParams(
            collective_id=0, has_side_effects=True, vmem_limit_bytes=24 * 1024 * 1024
        ),
    )(*[pltpu.with_memory_space_constraint(operand, pltpu.HBM) for operand in operands])
    partial_image = pl.pallas_call(
        image_kernel,
        out_shape=jax.ShapeDtypeStruct((depth, XW), jnp.float32),
        in_specs=[vmem] * 4,
        out_specs=vmem,
        scratch_shapes=[pltpu.VMEM((WIN, 2 * STEPS, XW, LANES), jnp.bfloat16)],
        compiler_params=pltpu.CompilerParams(vmem_limit_bytes=24 * 1024 * 1024),
    )(*tables)
    if lax.axis_size("offset") == 1:
        return partial_image
    return lax.psum_scatter(partial_image, "offset", scatter_dimension=0, tiled=True)


def solution(mesh):
    return jax.shard_map(
        shards,
        mesh=mesh,
        in_specs=(
            P("offset", "slab", None),
            P("offset", "slab", None),
            P("offset", "slab"),
            P("offset", "slab", None, None, None),
            P("offset", "slab", None, None, None),
            P("offset", None, None, None),
            P(),
        ),
        out_specs=P("offset", "slab"),
        check_vma=False,
    )
```

```python
import functools
import math

import jax
import jax.numpy as jnp
import ml_dtypes
import numpy as np
from jax import lax
from jax.experimental import pallas as pl
from jax.experimental.pallas import tpu as pltpu
from jax.sharding import PartitionSpec as P

NT = 256
NF = 64
KLO = 8
P_SIZE = 16
BINS = 16
WIN = 7
XW = 128
HALF = (WIN - 1) // 2
STEPS = NF // KLO
LANES = KLO * P_SIZE

slow_step = 0.25
width_scale = 200.0

def order(i):
    return HALF + (i + 1) // 2 * (1 - 2 * (i % 2))


OTHERS = [order(i) for i in range(1, WIN)]


def halves(table):
    high = table.astype(ml_dtypes.bfloat16)
    low = (table - high.astype(np.float64)).astype(ml_dtypes.bfloat16)
    return high, low


def dft_halves():
    turns = np.outer(np.arange(NT), np.arange(NF) + KLO) % NT * (2.0 * np.pi / NT)
    return np.concatenate(halves(np.concatenate([np.cos(turns), -np.sin(turns)], axis=1)), axis=1)


def by_chunk(table):
    rows = table.shape[0]
    return table.reshape(rows, 2, STEPS, LANES).transpose(2, 1, 0, 3).reshape(-1, rows, LANES)


def slant_halves():
    omega = (np.arange(NF) + KLO) * (2.0 * np.pi / NT)
    slow = (np.arange(P_SIZE) - (P_SIZE - 1) / 2.0) * slow_step
    place = np.arange(BINS) - (BINS - 1) / 2.0
    phase = place[:, None] * (omega[:, None] * slow[None, :]).reshape(1, -1)
    table = by_chunk(np.concatenate([np.cos(phase), np.sin(phase)], axis=1))
    return np.concatenate(halves(table), axis=1)


def spread_table():
    return by_chunk(np.repeat(np.eye(2 * NF), P_SIZE, axis=1)).astype(ml_dtypes.bfloat16)


def fit_even(values, degree):
    nodes = 0.125 - 0.125 * np.cos((np.arange(400) + 0.5) * np.pi / 400)
    poly = np.polynomial.chebyshev.Chebyshev.fit(nodes, values(np.sqrt(nodes)), degree, domain=[0, 0.25])
    return [float(c) for c in poly.convert(kind=np.polynomial.Polynomial).coef]


COS_FIT = fit_even(lambda y: np.cos(2 * np.pi * y), 7)
SIN_FIT = fit_even(lambda y: np.sin(2 * np.pi * y) / y, 6)


def horner(fit, s):
    total = jnp.full_like(s, fit[-1])
    for c in fit[-2::-1]:
        total = total * s + c
    return total


def turn(y):
    y = y - jnp.floor(y + 0.5)
    s = y * y
    return horner(COS_FIT, s), horner(SIN_FIT, s) * y


def pair(ref, at):
    return jnp.concatenate([ref[at], ref[at + 1]], axis=1)


def kernel(
    slabs, scale,
    traces_in, ids_in, bins_in, dft_in, slant_in, spread_in, times_in, amps_in, lateral_in, footprint_in,
    u, gauss, step, beams,
    traces, ids, bins, dft, slant, spread, lateral, footprint,
    rays, rays_here, sums, send, arrived,
    load_sem, send_sem, recv_sem, ray_send, ray_recv, beam_send, beam_recv,
):
    me = lax.axis_index("slab")
    parts = u.shape[1]

    def slab_at(k):
        return lax.rem(me + k, slabs)

    loads = [
        pltpu.make_async_copy(source, held, load_sem.at[i])
        for i, (source, held) in enumerate(
            (
                (traces_in.at[0], traces),
                (dft_in, dft),
                (ids_in, ids),
                (bins_in, bins),
                (slant_in, slant),
                (spread_in, spread),
                (times_in.at[0, 0], rays.at[:, 0]),
                (amps_in.at[0, 0], rays.at[:, 1]),
                (lateral_in.at[0], lateral),
                (footprint_in, footprint),
            )
        )
    ]
    for load in loads:
        load.start()

    barrier = pltpu.get_barrier_semaphore()

    def greet(k, carry):
        pl.semaphore_signal(barrier, inc=1, device_id={"slab": slab_at(k)}, device_id_type=pl.DeviceIdType.MESH)
        return carry

    lax.fori_loop(1, slabs, greet, 0)

    def block_copies(first, count):
        return pltpu.make_async_remote_copy(
            src_ref=send.at[pl.ds(slab_at(first), count)] if count == 1 else send.at[pl.ds(0, count)],
            dst_ref=arrived.at[pl.ds(first, count)],
            send_sem=send_sem,
            recv_sem=recv_sem,
            device_id={"slab": slab_at(first)},
            device_id_type=pl.DeviceIdType.MESH,
        )

    def start_block(k, carry):
        block_copies(k, 1).start()
        return carry

    def ray_copy(w):
        return pltpu.make_async_remote_copy(
            src_ref=rays.at[w],
            dst_ref=rays_here.at[w],
            send_sem=ray_send.at[w],
            recv_sem=ray_recv.at[w],
            device_id={"slab": slab_at(slabs + w - HALF)},
            device_id_type=pl.DeviceIdType.MESH,
        )

    def beam_copy(w):
        return pltpu.make_async_remote_copy(
            src_ref=beams.at[HALF],
            dst_ref=beams.at[w],
            send_sem=beam_send.at[w],
            recv_sem=beam_recv.at[w],
            device_id={"slab": slab_at(slabs + w - HALF)},
            device_id_type=pl.DeviceIdType.MESH,
        )

    def goes(w):
        target = me + (w - HALF)
        return (target >= 0) & (target < slabs)

    def comes(w):
        source = me - (w - HALF)
        return (source >= 0) & (source < slabs)

    def send_rays(slots):
        for w in slots:

            @pl.when(goes(w))
            def _():
                ray_copy(w).start()

    for load in loads[:4]:
        load.wait()
    spectrum = jnp.dot(traces[...], dft[...], preferred_element_type=jnp.float32)
    spectrum = spectrum[:, : 2 * NF] + spectrum[:, 2 * NF :]
    spec_high = spectrum.astype(jnp.bfloat16)
    spec_low = (spectrum - spec_high.astype(jnp.float32)).astype(jnp.bfloat16)
    spec = jnp.concatenate([spec_high, spec_low], axis=1)
    count = spec.shape[0]
    bin_row = lax.broadcasted_iota(jnp.int32, (2 * BINS, count), 0) % BINS
    bin_hot = jnp.where(bin_row == bins[...], 1.0, 0.0).T.astype(jnp.bfloat16)
    id_row = lax.broadcasted_iota(jnp.int32, (slabs, count), 0)
    id_hot = jnp.where(id_row == ids[...], 1.0, 0.0).astype(jnp.bfloat16)
    id_hot = jnp.concatenate([id_hot, id_hot], axis=1)
    for load in loads[4:8]:
        load.wait()

    pl.semaphore_wait(barrier, slabs - 1)
    send_rays(OTHERS[:3])
    for w in OTHERS:

        @pl.when(jnp.logical_not(comes(w)))
        def _():
            rays_here[w] = rays[w]
            beams[w] = jnp.zeros_like(beams[w])

    for chunk in range(STEPS):
        spread_wide = pair(spread, 2 * chunk)
        spec_wide = jnp.dot(
            spec,
            jnp.concatenate([spread_wide, spread_wide], axis=0),
            preferred_element_type=jnp.float32,
        )
        turn_wide = jnp.dot(bin_hot, pair(slant, 2 * chunk), preferred_element_type=jnp.float32)
        spec_re, spec_im = spec_wide[:, :LANES], spec_wide[:, LANES:]
        cosine, sine = turn_wide[:, :LANES], turn_wide[:, LANES:]
        terms = jnp.concatenate(
            [spec_re * cosine + spec_im * sine, spec_im * cosine - spec_re * sine], axis=1
        )
        high = terms.astype(jnp.bfloat16)
        low = (terms - high.astype(jnp.float32)).astype(jnp.bfloat16)
        partial = jnp.dot(
            id_hot, jnp.concatenate([high, low], axis=0), preferred_element_type=jnp.float32
        )
        sums[:, 2 * chunk, :] = partial[:, :LANES] * scale
        sums[:, 2 * chunk + 1, :] = partial[:, LANES:] * scale
    send[...] = sums[...].astype(jnp.bfloat16)
    lax.fori_loop(1, slabs, start_block, 0)
    send_rays(OTHERS[3:])

    def make_u(w, held):
        for part in range(parts):
            z = slice(part * 128, (part + 1) * 128)
            make_u_part(w, part, held[w, 0, :, z], held[w, 1, :, z])

    def make_u_part(w, part, t, a):
        cos8, sin8 = turn(t * (KLO / NT))
        cos1, sin1 = turn(t * (1.0 / NT))
        twice = 2.0 * cos8
        re, im = a, jnp.zeros_like(a)
        for b in range(KLO):
            if b:
                re, im = re * cos1 + im * sin1, im * cos1 - re * sin1
            last_re, last_im = re, im
            now_re, now_im = re * cos8 + im * sin8, im * cos8 - re * sin8
            for chunk in range(STEPS):
                at = 2 * chunk * LANES + b * P_SIZE
                u[w, part, at : at + P_SIZE, :] = now_re.astype(jnp.bfloat16)
                u[w, part, at + LANES : at + LANES + P_SIZE, :] = now_im.astype(jnp.bfloat16)
                if chunk < STEPS - 1:
                    now_re, last_re = twice * now_re - last_re, now_re
                    now_im, last_im = twice * now_im - last_im, now_im

    lane = lax.broadcasted_iota(jnp.int32, (1, LANES), 1)
    place = lax.broadcasted_iota(jnp.int32, (XW, LANES), 0).astype(jnp.float32)
    slow_row = lax.broadcasted_iota(jnp.int32, (P_SIZE, LANES), 0)
    slow_lane = lax.broadcasted_iota(jnp.int32, (P_SIZE, LANES), 1) % P_SIZE
    rate = -2.0 * math.pi / NT / width_scale * math.log2(math.e)
    rates = (lane // P_SIZE + KLO).astype(jnp.float32) * rate

    def pick(values, w):
        centre = jnp.clip(me - (w - HALF), 0, slabs - 1)
        held = lax.broadcasted_iota(jnp.int32, values.shape, 1) == centre
        return jnp.sum(jnp.where(held, values, 0.0), axis=1, keepdims=True)

    def make_gauss(w):
        axis = pick(lateral[w], w)
        axis = jnp.sum(jnp.where(slow_row == slow_lane, axis, 0.0), axis=0, keepdims=True)
        ends = pick(footprint[w].astype(jnp.float32), w)
        off = place - axis
        off = jnp.where((place >= ends[0:1]) & (place < ends[1:2]), off * off, 1e9)
        gauss[w] = jnp.exp2(off * rates) * (1.0 / math.sqrt(P_SIZE * NF))
        step[w] = jnp.exp2(off * (KLO * rate))

    def take_rays(i, carry):
        w = order(i)

        @pl.when(comes(w) & (w != HALF))
        def _():
            ray_copy(w).wait_recv()

        make_u(w, rays_here)
        return carry

    rays_here[HALF] = rays[HALF]
    for load in loads[8:]:
        load.wait()
    for w in range(WIN):
        make_gauss(w)
    lax.fori_loop(0, 4, take_rays, 0)

    arrived[0] = send[me]
    block_copies(1, slabs - 1).wait_recv()
    own = jnp.sum(arrived[...].astype(jnp.float32), axis=0)
    beams[HALF] = own.astype(jnp.bfloat16)
    for w in OTHERS:

        @pl.when(goes(w))
        def _():
            beam_copy(w).start()

    lax.fori_loop(4, WIN, take_rays, 0)
    for w in OTHERS:

        @pl.when(comes(w))
        def _():
            beam_copy(w).wait_recv()

    block_copies(1, slabs - 1).wait_send()
    for w in OTHERS:

        @pl.when(goes(w))
        def _():
            ray_copy(w).wait_send()
            beam_copy(w).wait_send()


def image_kernel(u, gauss, step, beams, image, v):
    total = jnp.zeros((XW, image.shape[0]), jnp.float32)
    for w in range(WIN):
        here = beams[w].astype(jnp.float32)
        g = gauss[w]
        for chunk in range(STEPS):
            if chunk:
                g = g * step[w]
            for at in (2 * chunk, 2 * chunk + 1):
                v[w, at] = (g * here[at : at + 1]).astype(jnp.bfloat16)
        total += jnp.dot(
            jnp.concatenate([v[w, at] for at in range(2 * STEPS)], axis=1),
            jnp.concatenate([u[w, part] for part in range(u.shape[1])], axis=1),
            preferred_element_type=jnp.float32,
        )
    image[...] = total.T


def shards(traces, centre_ids, midpoint_bins, ray_times, ray_amps, beam_lateral, footprint):
    slabs = lax.axis_size("slab")
    count = traces.shape[1]
    depth = ray_times.shape[4]
    columns = 2 * NF * P_SIZE
    operands = (
        traces,
        centre_ids.reshape(1, count),
        midpoint_bins,
        jnp.asarray(dft_halves()),
        jnp.asarray(slant_halves()),
        jnp.asarray(spread_table()),
        ray_times,
        ray_amps,
        beam_lateral.transpose(0, 2, 3, 1),
        footprint.transpose(1, 2, 0),
    )
    vmem = pl.BlockSpec(memory_space=pltpu.VMEM)
    tables = pl.pallas_call(
        functools.partial(kernel, slabs, 1.0 / math.sqrt(NT * count)),
        out_shape=[
            jax.ShapeDtypeStruct((WIN, depth // 128, columns, 128), jnp.bfloat16),
            jax.ShapeDtypeStruct((WIN, XW, LANES), jnp.float32),
            jax.ShapeDtypeStruct((WIN, XW, LANES), jnp.float32),
            jax.ShapeDtypeStruct((WIN, 2 * STEPS, LANES), jnp.bfloat16),
        ],
        in_specs=[pl.BlockSpec(memory_space=pltpu.HBM)] * 10,
        out_specs=[vmem] * 4,
        scratch_shapes=[
            pltpu.VMEM((count, NT), jnp.bfloat16),
            pltpu.VMEM((1, count), jnp.int32),
            pltpu.VMEM((1, count), jnp.int32),
            pltpu.VMEM((NT, 4 * NF), jnp.bfloat16),
            pltpu.VMEM((2 * STEPS, 2 * BINS, LANES), jnp.bfloat16),
            pltpu.VMEM((2 * STEPS, 2 * NF, LANES), jnp.bfloat16),
            pltpu.VMEM((WIN, P_SIZE, slabs), jnp.float32),
            pltpu.VMEM((WIN, 2, slabs), jnp.int32),
            pltpu.VMEM((WIN, 2, P_SIZE, depth), jnp.float32),
            pltpu.VMEM((WIN, 2, P_SIZE, depth), jnp.float32),
            pltpu.VMEM((slabs, 2 * STEPS, LANES), jnp.float32),
            pltpu.VMEM((slabs, 2 * STEPS, LANES), jnp.bfloat16),
            pltpu.VMEM((slabs, 2 * STEPS, LANES), jnp.bfloat16),
            pltpu.SemaphoreType.DMA((10,)),
            pltpu.SemaphoreType.DMA,
            pltpu.SemaphoreType.DMA,
            pltpu.SemaphoreType.DMA((WIN,)),
            pltpu.SemaphoreType.DMA((WIN,)),
            pltpu.SemaphoreType.DMA((WIN,)),
            pltpu.SemaphoreType.DMA((WIN,)),
        ],
        compiler_params=pltpu.CompilerParams(
            collective_id=0, has_side_effects=True, vmem_limit_bytes=24 * 1024 * 1024
        ),
    )(*[pltpu.with_memory_space_constraint(operand, pltpu.HBM) for operand in operands])
    partial_image = pl.pallas_call(
        image_kernel,
        out_shape=jax.ShapeDtypeStruct((depth, XW), jnp.float32),
        in_specs=[vmem] * 4,
        out_specs=vmem,
        scratch_shapes=[pltpu.VMEM((WIN, 2 * STEPS, XW, LANES), jnp.bfloat16)],
        compiler_params=pltpu.CompilerParams(vmem_limit_bytes=24 * 1024 * 1024),
    )(*tables)
    if lax.axis_size("offset") == 1:
        return partial_image
    return lax.psum_scatter(partial_image, "offset", scatter_dimension=0, tiled=True)


def solution(mesh):
    return jax.shard_map(
        shards,
        mesh=mesh,
        in_specs=(
            P("offset", "slab", None),
            P("offset", "slab", None),
            P("offset", "slab"),
            P("offset", "slab", None, None, None),
            P("offset", "slab", None, None, None),
            P("offset", None, None, None),
            P(),
        ),
        out_specs=P("offset", "slab"),
        check_vma=False,
    )
```
